1024 devices in a mesh: col: 64 (over y_hi, z, core), red: 16 (over y_lo, x).
Axes of the slice: x: 8, y: 8 (y_hi: 4, y_lo: 2; y = y_hi * 2 + y_lo), z: 8, core: 2. Of those that a mesh axis runs over, the one named last changes fastest.
Arguments:
- amplitudes: bfloat16 [128, 1048576], P(None, ('red', 'col')), may hold values from -6 to 6
- block_tiles: bfloat16 [16, 64, 64, 24576], P('red', 'col'), may hold values from -0.029907227 to 0.029907227
- block_rows: int32 [16, 64, 48], P('red', 'col'), may hold values from 0 to 1023, as said below
- tile_mask: int32 [16, 64, 48, 8], P('red', 'col'), may hold values 0 or 1
- block_counts: int32 [16, 64], P('red', 'col'), may hold values from 40 to 48, as said below
Outputs:
- ladder: float32 [128, 32768], P(None, 'col')
The draws below stay inside these ranges and needn't reach their ends.
Inputs may be any that keep to these rules, and one draw needn't show every extreme that they name: In every device's list, at most 2 slots name tile rows of one range of 16 rows (block_rows // 16), and some range gets exactly 2 within the first 40 slots. `block_counts`: some device has 48 live slots and some 40.
All inputs are finite; a program needn't handle non-finite values. No bound on the sum of `tile_mask` on one device may be relied on, other than what follows from the above.
Results may differ from the reference program's by a relative error of at most 0.0003.
Values may be sent and summed in bfloat16 or wider, within the bound.
No kernel may reach another device: no remote copies, remote signals or barrier semaphores. Data moves between devices by JAX's collectives and lax.ppermute only.
A program may use at most 32 MiB of HBM per device.

```python
import jax
import jax.numpy as jnp
from jax import lax

ROWS = 128
COLS_DEV = 512
K = 1048576
BLOCK = 64
NB_MAX = 48
NB_MIN = 40
KBD = 16
CBD = 8
CAP = 2
COLS = 32768
N_COL = 64
N_RED = 16


def draw_block_counts(key, part):
    key = jax.random.fold_in(key, 11)
    first, second, third, fourth = jax.random.split(key, 4)
    devices_all = N_RED * N_COL
    spread = NB_MAX - NB_MIN
    left_part = jax.random.randint(first, (devices_all,), 0, spread + 1)
    right_part = jax.random.randint(second, (devices_all,), 0, spread + 1)
    counts = NB_MAX - left_part * right_part // max(spread, 1)
    busiest = jax.random.randint(third, (), 0, devices_all)
    lightest = (busiest + 1 + jax.random.randint(fourth, (), 0, devices_all - 1)) % devices_all
    counts = counts.at[busiest].set(NB_MAX)
    counts = counts.at[lightest].set(NB_MIN)
    return counts.reshape(N_RED, N_COL).astype(jnp.int32)


def one_list(key):
    keys = jax.random.split(key, 5)
    first_peer = jax.random.randint(keys[0], (), 0, N_COL)
    pool = jax.random.permutation(keys[1], CAP * (N_COL - 1))[:NB_MAX - CAP]
    others = (first_peer + 1 + pool % (N_COL - 1)) % N_COL
    owners = jnp.concatenate([jnp.full((CAP,), first_peer, jnp.int32), others.astype(jnp.int32)])
    order = jnp.concatenate([jax.random.permutation(keys[2], NB_MIN), NB_MIN + jax.random.permutation(keys[3], NB_MAX - NB_MIN)])
    owners = owners[order]
    within = jax.random.randint(keys[4], (NB_MAX,), 0, KBD)
    return (owners * KBD + within).astype(jnp.int32)


def draw_block_rows(key, part):
    key = jax.random.fold_in(key, 23)
    device_keys = jax.random.split(key, N_RED * N_COL)
    lists = jax.vmap(one_list)(device_keys)
    return lists.reshape(N_RED, N_COL, NB_MAX)


def with_ends(entries, key, low, high):
    spot = [jax.random.randint(jax.random.fold_in(key, axis), (), 0, length) for axis, length in enumerate(entries.shape)]
    main_axis = entries.shape.index(max(entries.shape))
    neighbour = spot[:main_axis] + [(spot[main_axis] + 1) % entries.shape[main_axis]] + spot[main_axis + 1:]
    return entries.at[tuple(spot)].set(low).at[tuple(neighbour)].set(high)


def block_levels(stream_key, dims, cuts, low, top_value):
    def one(axis_at, shards_of):
        heights = jax.random.uniform(jax.random.fold_in(jax.random.fold_in(stream_key, 6), axis_at), (shards_of,), jnp.float32, low / len(cuts), top_value / len(cuts))
        return jnp.repeat(jnp.exp(heights), dims[axis_at] // shards_of).reshape((-1,) + (1,) * (len(dims) - axis_at - 1))

    factor_of = one(*cuts[0])
    for cut in cuts[1:]:
        factor_of = factor_of * one(*cut)
    return factor_of


def normal_values(rng, dims, scale, reach, pieces=(), kind=jnp.bfloat16):
    result = scale * jax.random.normal(rng, dims, jnp.float32)
    if pieces:
        result = result * block_levels(rng, dims, pieces, -0.22, 0.18)
    return jnp.clip(result, -reach, reach).astype(kind)


def setup_inputs(seed: int = 0) -> dict:
    streams_of = jax.random.split(jax.random.key(seed), 6)
    amplitudes = normal_values(streams_of[0], (ROWS, K), 1.0, 6.0, ((1, 1024),))
    block_tiles = normal_values(streams_of[1], (N_RED, N_COL, BLOCK, NB_MAX * COLS_DEV), 0.005, 0.029907227, ((0, 16), (1, 64)))
    block_rows = draw_block_rows(jax.random.fold_in(streams_of[5], 71), 0)
    tile_mask = with_ends((jax.random.randint(streams_of[3], (N_RED, N_COL, NB_MAX, CBD), 0, 4) < 3).astype(jnp.int32), jax.random.fold_in(streams_of[3], 1), 0, 1)
    block_counts = draw_block_counts(jax.random.fold_in(streams_of[5], 71), 0)
    return dict(amplitudes=amplitudes, block_tiles=block_tiles, block_rows=block_rows, tile_mask=tile_mask, block_counts=block_counts)


def reference(amplitudes, block_tiles, block_rows, tile_mask, block_counts):
    blocked = amplitudes.reshape(ROWS, K // 64, 64)

    def one_red(carry, items):
        tile_data, row_ids, mask, counts, index = items
        global_rows = (index * KBD * N_COL + row_ids).astype(jnp.int32).reshape(-1)
        picked = jnp.take(blocked, global_rows, axis=1).reshape(ROWS, N_COL, NB_MAX, 64).astype(jnp.float32)
        alive = (jnp.arange(NB_MAX)[None, :] < counts[:, None]).astype(jnp.float32)
        picked = picked * alive[None, :, :, None]
        col_mask = jnp.repeat(mask.astype(jnp.float32), 64, axis=-1)
        tiles = tile_data.reshape(N_COL, 64, NB_MAX, COLS_DEV).astype(jnp.float32) * col_mask[:, None, :, :]
        contrib = jnp.einsum("rcsk,cksj->rcj", picked, tiles)
        return carry + contrib, None

    start = jnp.zeros((ROWS, N_COL, COLS_DEV), jnp.float32)
    summed, unused = lax.scan(one_red, start, (block_tiles, block_rows, tile_mask, block_counts, jnp.arange(N_RED, dtype=jnp.int32)))
    return summed.reshape(ROWS, COLS)
```

```python
import jax
import jax.numpy as jnp
from jax import lax
from jax.sharding import PartitionSpec as P

BLOCK = 64
CAP = 2


def peer_rank(owners):
    width = owners.shape[0]
    same = owners[:, None] == owners[None, :]
    earlier = jnp.arange(width)[None, :] < jnp.arange(width)[:, None]
    return jnp.sum((same & earlier).astype(jnp.int32), axis=-1)


def body(amplitudes, block_tiles, block_rows, tile_mask, block_counts):
    row_ids = block_rows[0, 0]
    slots = row_ids.shape[0]
    col_tiles = tile_mask.shape[-1]
    cols_here = col_tiles * BLOCK
    rows = amplitudes.shape[0]
    blocks_here = amplitudes.shape[1] // BLOCK
    n_col = lax.axis_size("col")
    n_red = lax.axis_size("red")
    alive = jnp.arange(slots) < block_counts[0, 0]

    owners = row_ids // blocks_here
    place = owners * CAP + peer_rank(owners)
    here = (place[None, :] == jnp.arange(n_col * CAP)[:, None]) & alive[None, :]
    ask = jnp.sum(jnp.where(here, (row_ids % blocks_here + 1)[None, :], 0), axis=-1)
    asked = lax.all_to_all(ask.reshape(n_col, CAP), "col", split_axis=0, concat_axis=0, tiled=True)

    blocks = amplitudes.T.reshape(blocks_here, BLOCK, rows)
    outgoing = blocks[jnp.maximum(asked - 1, 0)]
    incoming = lax.all_to_all(outgoing, "col", split_axis=0, concat_axis=0, tiled=True)

    tile_data = block_tiles[0, 0].reshape(BLOCK, slots, cols_here)
    keep = jnp.repeat(tile_mask[0, 0], BLOCK, axis=1).astype(jnp.bfloat16)
    masked = tile_data * keep[None, :, :]
    picked = incoming.reshape(n_col * CAP, BLOCK, rows)[place]
    picked = picked * alive.astype(jnp.bfloat16)[:, None, None]
    partial_value = jnp.einsum("skr,ksj->rj", picked, masked, preferred_element_type=jnp.float32)

    slices = partial_value.reshape(n_red, rows // n_red, cols_here)
    gathered = lax.all_to_all(slices, "red", split_axis=0, concat_axis=0, tiled=True)
    mine = jnp.sum(gathered, axis=0)
    copies = jnp.broadcast_to(mine[None], gathered.shape)
    whole = lax.all_to_all(copies, "red", split_axis=0, concat_axis=0, tiled=True)
    return whole.reshape(rows, cols_here)


def solution(mesh):
    placed = (
        P(None, ("red", "col")),
        P("red", "col", None, None),
        P("red", "col", None),
        P("red", "col", None, None),
        P("red", "col"),
    )
    return jax.shard_map(
        body, mesh=mesh, in_specs=placed, out_specs=P(None, "col"), check_vma=False
    )
```

```python
import jax
import jax.numpy as jnp
from jax import lax
from jax.experimental import pallas as pl
from jax.experimental.pallas import tpu as pltpu
from jax.sharding import PartitionSpec as P

BLOCK = 64
CAP = 2
GROUP = 4


def peer_rank(owners):
    width = owners.shape[0]
    same = owners[:, None] == owners[None, :]
    earlier = jnp.arange(width)[None, :] < jnp.arange(width)[:, None]
    return jnp.sum((same & earlier).astype(jnp.int32), axis=-1)


def contract_kernel(place, blocks, tiles, keep, out, a_buf, w_buf, a_sem, w_sem):
    slots, cols = keep.shape
    groups = slots // GROUP

    def a_copy(s):
        return pltpu.make_async_copy(
            blocks.at[place[s]], a_buf.at[pl.ds(s * BLOCK, BLOCK)], a_sem.at[s]
        )

    def w_copy(s):
        return pltpu.make_async_copy(
            tiles.at[:, pl.ds(s * cols, cols)], w_buf.at[pl.ds(s * BLOCK, BLOCK)], w_sem.at[s]
        )

    for s in range(slots):
        w_copy(s).start()
        a_copy(s).start()
    total = jnp.zeros(out.shape, jnp.float32)
    for g in range(groups):
        parts = []
        for s in range(g * GROUP, (g + 1) * GROUP):
            a_copy(s).wait()
            w_copy(s).wait()
            parts.append(w_buf[pl.ds(s * BLOCK, BLOCK), :] * keep[pl.ds(s, 1), :])
        lhs = a_buf[pl.ds(g * GROUP * BLOCK, GROUP * BLOCK), :]
        total += lax.dot_general(
            lhs,
            jnp.concatenate(parts, axis=0),
            (((0,), (0,)), ((), ())),
            preferred_element_type=jnp.float32,
        )
    out[...] = total


def contract(place, blocks, tiles, keep):
    slots, cols = keep.shape
    rows = blocks.shape[-1]
    return pl.pallas_call(
        contract_kernel,
        out_shape=jax.ShapeDtypeStruct((rows, cols), jnp.float32),
        in_specs=[
            pl.BlockSpec(memory_space=pltpu.SMEM),
            pl.BlockSpec(memory_space=pl.ANY),
            pl.BlockSpec(memory_space=pl.ANY),
            pl.BlockSpec(memory_space=pltpu.VMEM),
        ],
        out_specs=pl.BlockSpec(memory_space=pltpu.VMEM),
        scratch_shapes=[
            pltpu.VMEM((slots * BLOCK, rows), jnp.bfloat16),
            pltpu.VMEM((slots * BLOCK, cols), jnp.bfloat16),
            pltpu.SemaphoreType.DMA((slots,)),
            pltpu.SemaphoreType.DMA((slots,)),
        ],
        compiler_params=pltpu.CompilerParams(vmem_limit_bytes=16 * 1024 * 1024),
        cost_estimate=pl.CostEstimate(
            flops=2 * slots * BLOCK * rows * cols, bytes_accessed=4 * 1024 * 1024, transcendentals=0
        ),
    )(place, blocks, tiles, keep)


def body(amplitudes, block_tiles, block_rows, tile_mask, block_counts):
    row_ids = block_rows[0, 0]
    slots = row_ids.shape[0]
    col_tiles = tile_mask.shape[-1]
    cols_here = col_tiles * BLOCK
    rows = amplitudes.shape[0]
    blocks_here = amplitudes.shape[1] // BLOCK
    n_col = lax.axis_size("col")
    n_red = lax.axis_size("red")
    alive = jnp.arange(slots) < block_counts[0, 0]

    owners = row_ids // blocks_here
    place = owners * CAP + peer_rank(owners)
    here = (place[None, :] == jnp.arange(n_col * CAP)[:, None]) & alive[None, :]
    ask = jnp.sum(jnp.where(here, (row_ids % blocks_here + 1)[None, :], 0), axis=-1)
    asked = lax.all_to_all(ask.reshape(n_col, CAP), "col", split_axis=0, concat_axis=0, tiled=True)

    blocks = amplitudes.T.reshape(blocks_here, BLOCK, rows)
    outgoing = blocks[jnp.maximum(asked - 1, 0)]
    incoming = lax.all_to_all(outgoing, "col", split_axis=0, concat_axis=0, tiled=True)

    keep = jnp.repeat(tile_mask[0, 0] * alive[:, None], BLOCK, axis=1).astype(jnp.bfloat16)
    partial_value = contract(
        jnp.clip(place, 0, n_col * CAP - 1),
        incoming.reshape(n_col * CAP, BLOCK, rows),
        block_tiles[0, 0],
        keep,
    )

    slices = partial_value.reshape(n_red, rows // n_red, cols_here)
    gathered = lax.all_to_all(slices, "red", split_axis=0, concat_axis=0, tiled=True)
    mine = jnp.sum(gathered, axis=0)
    copies = jnp.broadcast_to(mine[None], gathered.shape)
    whole = lax.all_to_all(copies, "red", split_axis=0, concat_axis=0, tiled=True)
    return whole.reshape(rows, cols_here)


def solution(mesh):
    placed = (
        P(None, ("red", "col")),
        P("red", "col", None, None),
        P("red", "col", None),
        P("red", "col", None, None),
        P("red", "col"),
    )
    return jax.shard_map(
        body, mesh=mesh, in_specs=placed, out_specs=P(None, "col"), check_vma=False
    )
```

```python
import jax
import jax.numpy as jnp
from jax import lax
from jax.experimental import pallas as pl
from jax.experimental.pallas import tpu as pltpu
from jax.sharding import PartitionSpec as P

BLOCK = 64
CAP = 2
GROUP = 4


def peer_rank(owners):
    width = owners.shape[0]
    same = owners[:, None] == owners[None, :]
    earlier = jnp.arange(width)[None, :] < jnp.arange(width)[:, None]
    return jnp.sum((same & earlier).astype(jnp.int32), axis=-1)


def stack_kernel(tiles, keep, out, buf, sem):
    slots, cols = keep.shape
    chunks, _, width = buf.shape
    each = slots // chunks

    def copy(i):
        return pltpu.make_async_copy(tiles.at[:, pl.ds(i * width, width)], buf.at[i], sem.at[i])

    for i in range(chunks):
        copy(i).start()
    for i in range(chunks):
        copy(i).wait()
        for j in range(each):
            s = i * each + j
            out[pl.ds(s * BLOCK, BLOCK), :] = buf[i, :, pl.ds(j * cols, cols)] * keep[pl.ds(s, 1), :]


def stack(tiles, keep):
    slots, cols = keep.shape
    chunks = slots // GROUP
    return pl.pallas_call(
        stack_kernel,
        out_shape=jax.ShapeDtypeStruct((slots * BLOCK, cols), tiles.dtype),
        in_specs=[
            pl.BlockSpec(memory_space=pl.ANY),
            pl.BlockSpec(memory_space=pltpu.VMEM),
        ],
        out_specs=pl.BlockSpec(memory_space=pltpu.VMEM),
        scratch_shapes=[
            pltpu.VMEM((chunks, BLOCK, GROUP * cols), tiles.dtype),
            pltpu.SemaphoreType.DMA((chunks,)),
        ],
        compiler_params=pltpu.CompilerParams(vmem_limit_bytes=16 * 1024 * 1024),
        cost_estimate=pl.CostEstimate(
            flops=slots * BLOCK * cols, bytes_accessed=4 * slots * BLOCK * cols, transcendentals=0
        ),
    )(tiles, keep)


def contract_kernel(place, blocks, weights, out):
    total = jnp.zeros(out.shape, jnp.float32)
    depth = GROUP * BLOCK
    for g in range(weights.shape[0] // depth):
        lhs = jnp.concatenate([blocks[place[g * GROUP + s]] for s in range(GROUP)], axis=0)
        total += lax.dot_general(
            lhs,
            weights[pl.ds(g * depth, depth), :],
            (((0,), (0,)), ((), ())),
            preferred_element_type=jnp.float32,
        )
    out[...] = total


def contract(place, blocks, weights):
    depth, cols = weights.shape
    rows = blocks.shape[-1]
    return pl.pallas_call(
        contract_kernel,
        out_shape=jax.ShapeDtypeStruct((rows, cols), jnp.float32),
        in_specs=[
            pl.BlockSpec(memory_space=pltpu.SMEM),
            pl.BlockSpec(memory_space=pltpu.VMEM),
            pl.BlockSpec(memory_space=pltpu.VMEM),
        ],
        out_specs=pl.BlockSpec(memory_space=pltpu.VMEM),
        compiler_params=pltpu.CompilerParams(vmem_limit_bytes=16 * 1024 * 1024),
        cost_estimate=pl.CostEstimate(
            flops=2 * depth * rows * cols, bytes_accessed=5 * 1024 * 1024, transcendentals=0
        ),
    )(place, blocks, weights)


def body(amplitudes, block_tiles, block_rows, tile_mask, block_counts):
    row_ids = block_rows[0, 0]
    slots = row_ids.shape[0]
    col_tiles = tile_mask.shape[-1]
    cols_here = col_tiles * BLOCK
    rows = amplitudes.shape[0]
    blocks_here = amplitudes.shape[1] // BLOCK
    n_col = lax.axis_size("col")
    n_red = lax.axis_size("red")
    alive = jnp.arange(slots) < block_counts[0, 0]

    owners = row_ids // blocks_here
    place = owners * CAP + peer_rank(owners)
    here = (place[None, :] == jnp.arange(n_col * CAP)[:, None]) & alive[None, :]
    ask = jnp.sum(jnp.where(here, (row_ids % blocks_here + 1)[None, :], 0), axis=-1)
    asked = lax.all_to_all(ask.reshape(n_col, CAP), "col", split_axis=0, concat_axis=0, tiled=True)

    blocks = amplitudes.T.reshape(blocks_here, BLOCK, rows)
    outgoing = blocks[jnp.maximum(asked - 1, 0)]
    incoming = lax.all_to_all(outgoing, "col", split_axis=0, concat_axis=0, tiled=True)

    keep = jnp.repeat(tile_mask[0, 0] * alive[:, None], BLOCK, axis=1).astype(jnp.bfloat16)
    weights = stack(block_tiles[0, 0], keep)
    partial_value = contract(
        jnp.clip(place, 0, n_col * CAP - 1), incoming.reshape(n_col * CAP, BLOCK, rows), weights
    )

    slices = partial_value.reshape(n_red, rows // n_red, cols_here)
    gathered = lax.all_to_all(slices, "red", split_axis=0, concat_axis=0, tiled=True)
    mine = jnp.sum(gathered, axis=0)
    copies = jnp.broadcast_to(mine[None], gathered.shape)
    whole = lax.all_to_all(copies, "red", split_axis=0, concat_axis=0, tiled=True)
    return whole.reshape(rows, cols_here)


def solution(mesh):
    placed = (
        P(None, ("red", "col")),
        P("red", "col", None, None),
        P("red", "col", None),
        P("red", "col", None, None),
        P("red", "col"),
    )
    return jax.shard_map(
        body, mesh=mesh, in_specs=placed, out_specs=P(None, "col"), check_vma=False
    )
```

```python
import jax
import jax.numpy as jnp
from jax import lax
from jax.experimental import pallas as pl
from jax.experimental.pallas import tpu as pltpu
from jax.sharding import Mesh
from jax.sharding import PartitionSpec as P

BLOCK = 64
CAP = 2
GROUP = 4
AXES = ("y_hi1", "y_hi0", "z", "core", "y_lo", "x")
SIZES = (2, 2, 8, 2, 2, 8)
COL = AXES[:4]
RED = AXES[4:]
SERVERS = ("y_hi0", "z")


def peer_rank(owners):
    width = owners.shape[0]
    same = owners[:, None] == owners[None, :]
    earlier = jnp.arange(width)[None, :] < jnp.arange(width)[:, None]
    return jnp.sum((same & earlier).astype(jnp.int32), axis=-1)


def stack_kernel(tiles, keep, out, buf, sem):
    slots, cols = keep.shape
    chunks, _, width = buf.shape
    each = slots // chunks

    def copy(i):
        return pltpu.make_async_copy(tiles.at[:, pl.ds(i * width, width)], buf.at[i], sem.at[i])

    for i in range(chunks):
        copy(i).start()
    for i in range(chunks):
        copy(i).wait()
        for j in range(each):
            s = i * each + j
            out[pl.ds(s * BLOCK, BLOCK), :] = buf[i, :, pl.ds(j * cols, cols)] * keep[pl.ds(s, 1), :]


def stack(tiles, keep):
    slots, cols = keep.shape
    chunks = slots // GROUP
    return pl.pallas_call(
        stack_kernel,
        out_shape=jax.ShapeDtypeStruct((slots * BLOCK, cols), tiles.dtype),
        in_specs=[
            pl.BlockSpec(memory_space=pl.ANY),
            pl.BlockSpec(memory_space=pltpu.VMEM),
        ],
        out_specs=pl.BlockSpec(memory_space=pltpu.VMEM),
        scratch_shapes=[
            pltpu.VMEM((chunks, BLOCK, GROUP * cols), tiles.dtype),
            pltpu.SemaphoreType.DMA((chunks,)),
        ],
        compiler_params=pltpu.CompilerParams(vmem_limit_bytes=16 * 1024 * 1024),
        cost_estimate=pl.CostEstimate(
            flops=slots * BLOCK * cols, bytes_accessed=4 * slots * BLOCK * cols, transcendentals=0
        ),
    )(tiles, keep)


def contract_kernel(place, blocks, weights, out):
    total = jnp.zeros(out.shape, jnp.float32)
    depth = GROUP * BLOCK
    for g in range(weights.shape[0] // depth):
        lhs = jnp.concatenate([blocks[place[g * GROUP + s]] for s in range(GROUP)], axis=0)
        total += lax.dot_general(
            lhs,
            weights[pl.ds(g * depth, depth), :],
            (((0,), (0,)), ((), ())),
            preferred_element_type=jnp.float32,
        )
    out[...] = total


def contract(place, blocks, weights):
    depth, cols = weights.shape
    rows = blocks.shape[-1]
    return pl.pallas_call(
        contract_kernel,
        out_shape=jax.ShapeDtypeStruct((rows, cols), jnp.float32),
        in_specs=[
            pl.BlockSpec(memory_space=pltpu.SMEM),
            pl.BlockSpec(memory_space=pltpu.VMEM),
            pl.BlockSpec(memory_space=pltpu.VMEM),
        ],
        out_specs=pl.BlockSpec(memory_space=pltpu.VMEM),
        compiler_params=pltpu.CompilerParams(vmem_limit_bytes=16 * 1024 * 1024),
        cost_estimate=pl.CostEstimate(
            flops=2 * depth * rows * cols, bytes_accessed=5 * 1024 * 1024, transcendentals=0
        ),
    )(place, blocks, weights)


def pick_kernel(asked, *refs):
    *sources, out = refs
    each = len(sources) * CAP
    for slot in range(out.shape[0]):
        out[slot] = sources[slot % each // CAP][jnp.maximum(asked[slot] - 1, 0)]


def pick(asked, sources):
    slots = asked.shape[0]
    shape = (slots,) + sources[0].shape[1:]
    return pl.pallas_call(
        pick_kernel,
        out_shape=jax.ShapeDtypeStruct(shape, sources[0].dtype),
        in_specs=[pl.BlockSpec(memory_space=pltpu.SMEM)]
        + [pl.BlockSpec(memory_space=pltpu.VMEM)] * len(sources),
        out_specs=pl.BlockSpec(memory_space=pltpu.VMEM),
        compiler_params=pltpu.CompilerParams(vmem_limit_bytes=16 * 1024 * 1024),
        cost_estimate=pl.CostEstimate(
            flops=0, bytes_accessed=4 * slots * BLOCK * shape[-1], transcendentals=0
        ),
    )(asked, *sources)


def body(amplitudes, block_tiles, block_rows, tile_mask, block_counts):
    row_ids = block_rows[0, 0]
    slots = row_ids.shape[0]
    col_tiles = tile_mask.shape[-1]
    cols_here = col_tiles * BLOCK
    rows = amplitudes.shape[0]
    blocks_here = amplitudes.shape[1] // BLOCK
    n_servers = lax.axis_size(SERVERS)
    n_red = lax.axis_size(RED)
    alive = jnp.arange(slots) < block_counts[0, 0]

    own = amplitudes.T.reshape(blocks_here, BLOCK, rows)
    n_y = lax.axis_size(AXES[:2])
    n_core = lax.axis_size("core")
    opposite = [(y, n_y - 1 - y) for y in range(n_y)]
    across = [(c, n_core - 1 - c) for c in range(n_core)]
    both = [(y * n_core + c, (n_y - 1 - y) * n_core + n_core - 1 - c) for y in range(n_y) for c in range(n_core)]
    sources = [
        own,
        lax.ppermute(own, AXES[:2], opposite),
        lax.ppermute(own, "core", across),
        lax.ppermute(own, AXES[:2] + ("core",), both),
    ]

    owners = row_ids // blocks_here
    owner_core = owners % n_core
    owner_z = owners // n_core % lax.axis_size("z")
    owner_y = owners // (n_core * lax.axis_size("z"))
    flip = (owner_y // 2 != lax.axis_index("y_hi1")).astype(jnp.int32)
    server = (owner_y % 2 ^ flip) * lax.axis_size("z") + owner_z
    source = flip + 2 * (owner_core != lax.axis_index("core")).astype(jnp.int32)
    place = (server * len(sources) + source) * CAP + peer_rank(owners)
    n_places = n_servers * len(sources) * CAP

    here = (place[None, :] == jnp.arange(n_places)[:, None]) & alive[None, :]
    ask = jnp.sum(jnp.where(here, (row_ids % blocks_here + 1)[None, :], 0), axis=-1)
    ask = ask.reshape(n_servers, len(sources) * CAP)
    asked = lax.all_to_all(ask, SERVERS, split_axis=0, concat_axis=0, tiled=True)

    outgoing = pick(asked.reshape(n_places), sources)
    outgoing = outgoing.reshape(n_servers, len(sources) * CAP, BLOCK, rows)
    incoming = lax.all_to_all(outgoing, SERVERS, split_axis=0, concat_axis=0, tiled=True)

    keep = jnp.repeat(tile_mask[0, 0] * alive[:, None], BLOCK, axis=1).astype(jnp.bfloat16)
    weights = stack(block_tiles[0, 0], keep)
    partial_value = contract(
        jnp.clip(place, 0, n_places - 1), incoming.reshape(n_places, BLOCK, rows), weights
    )

    slices = partial_value.reshape(n_red, rows // n_red, cols_here)
    gathered = lax.all_to_all(slices, RED, split_axis=0, concat_axis=0, tiled=True)
    mine = jnp.sum(gathered, axis=0)
    copies = jnp.broadcast_to(mine[None], gathered.shape)
    whole = lax.all_to_all(copies, RED, split_axis=0, concat_axis=0, tiled=True)
    return whole.reshape(rows, cols_here)


def solution(mesh):
    fine = Mesh(mesh.devices.reshape(SIZES), AXES)
    placed = (
        P(None, RED + COL),
        P(RED, COL, None, None),
        P(RED, COL, None),
        P(RED, COL, None, None),
        P(RED, COL),
    )
    return jax.shard_map(
        body, mesh=fine, in_specs=placed, out_specs=P(None, COL), check_vma=False
    )
```

```python
import jax
import jax.numpy as jnp
from jax import lax
from jax.experimental import pallas as pl
from jax.experimental.pallas import tpu as pltpu
from jax.sharding import PartitionSpec as P

BLOCK = 64
HALF = 32
CAP = 2
GROUP = 4
NY = 4
NZ = 8
NCORE = 2
STEPS = 4
LIMIT = pltpu.CompilerParams(vmem_limit_bytes=16 * 1024 * 1024)


def col_index(y, z, core):
    return (y % NY * NZ + z % NZ) * NCORE + core


def server_groups():
    along_z = [[col_index(y, z, 0) for z in range(NZ)] for y in range(NY)]
    along_y = [
        [col_index(y, 2 * pair + odd, 1) for y in range(NY) for odd in range(2)]
        for pair in range(NZ // 2)
    ]
    return along_z + along_y


def step_pairs(step):
    pairs = []
    for y in range(NY):
        for z in range(NZ):
            pairs.append((col_index(y + step, z, 0), col_index(y, z, 0)))
            pairs.append((col_index(y, z + 2 * step, 1), col_index(y, z, 1)))
    return pairs


def swap_pairs():
    return [(i, i ^ 1) for i in range(NY * NZ * NCORE)]


def peer_rank(owners):
    width = owners.shape[-1]
    same = owners[..., :, None] == owners[..., None, :]
    earlier = jnp.arange(width)[None, :] < jnp.arange(width)[:, None]
    return jnp.sum((same & earlier).astype(jnp.int32), axis=-1)


def stack_kernel(mine, tiles, keep, out, buf, sem):
    slots, cols = keep.shape
    chunks, _, width = buf.shape
    each = slots // chunks

    def copy(i):
        return pltpu.make_async_copy(tiles.at[:, pl.ds(i * width, width)], buf.at[i], sem.at[i])

    for i in range(chunks):
        copy(i).start()
    for i in range(chunks):
        copy(i).wait()
        for part in range(2):
            half = mine[0] if part == 0 else 1 - mine[0]
            rows = pl.ds(pl.multiple_of(half * HALF, HALF), HALF)
            for j in range(each):
                s = i * each + j
                out[part, pl.ds(s * HALF, HALF), :] = (
                    buf[i, rows, pl.ds(j * cols, cols)] * keep[pl.ds(s, 1), :]
                )


def stack(mine, tiles, keep):
    slots, cols = keep.shape
    chunks = slots // GROUP
    return pl.pallas_call(
        stack_kernel,
        out_shape=jax.ShapeDtypeStruct((2, slots * HALF, cols), tiles.dtype),
        in_specs=[
            pl.BlockSpec(memory_space=pltpu.SMEM),
            pl.BlockSpec(memory_space=pl.ANY),
            pl.BlockSpec(memory_space=pltpu.VMEM),
        ],
        out_specs=pl.BlockSpec(memory_space=pltpu.VMEM),
        scratch_shapes=[
            pltpu.VMEM((chunks, BLOCK, GROUP * cols), tiles.dtype),
            pltpu.SemaphoreType.DMA((chunks,)),
        ],
        compiler_params=LIMIT,
        cost_estimate=pl.CostEstimate(
            flops=slots * BLOCK * cols, bytes_accessed=4 * slots * BLOCK * cols, transcendentals=0
        ),
    )(mine, tiles, keep)


def pick_kernel(asked, *refs):
    *sources, out = refs
    per_peer = STEPS * NCORE * CAP
    blocks_here = sources[0].shape[0] // NCORE
    for slot in range(out.shape[0]):
        step = slot % per_peer // (NCORE * CAP)
        core = slot // CAP % NCORE
        out[slot] = sources[step][core * blocks_here + jnp.maximum(asked[slot] - 1, 0)]


def pick(asked, sources):
    slots = asked.shape[0]
    shape = (slots,) + sources[0].shape[1:]
    return pl.pallas_call(
        pick_kernel,
        out_shape=jax.ShapeDtypeStruct(shape, sources[0].dtype),
        in_specs=[pl.BlockSpec(memory_space=pltpu.SMEM)]
        + [pl.BlockSpec(memory_space=pltpu.VMEM)] * len(sources),
        out_specs=pl.BlockSpec(memory_space=pltpu.VMEM),
        compiler_params=LIMIT,
        cost_estimate=pl.CostEstimate(
            flops=0, bytes_accessed=4 * slots * HALF * shape[-1], transcendentals=0
        ),
    )(asked, *sources)


def select_kernel(place, blocks, out):
    for s in range(out.shape[0]):
        out[s] = blocks[place[s]]


def select(place, blocks):
    slots = place.shape[0]
    shape = (slots,) + blocks.shape[1:]
    return pl.pallas_call(
        select_kernel,
        out_shape=jax.ShapeDtypeStruct(shape, blocks.dtype),
        in_specs=[
            pl.BlockSpec(memory_space=pltpu.SMEM),
            pl.BlockSpec(memory_space=pltpu.VMEM),
        ],
        out_specs=pl.BlockSpec(memory_space=pltpu.VMEM),
        compiler_params=LIMIT,
        cost_estimate=pl.CostEstimate(
            flops=0, bytes_accessed=2 * blocks.size, transcendentals=0
        ),
    )(place, blocks)


def contract_kernel(place, blocks, weights, *refs):
    *start, out = refs
    total = start[0][...] if start else jnp.zeros(out.shape, jnp.float32)
    half = 1 if start else 0
    each = 2 * GROUP
    depth = each * HALF
    for g in range(weights.shape[1] // depth):
        lhs = jnp.concatenate([blocks[place[g * each + s]] for s in range(each)], axis=0)
        total += lax.dot_general(
            lhs,
            weights[half, pl.ds(g * depth, depth), :],
            (((0,), (0,)), ((), ())),
            preferred_element_type=jnp.float32,
        )
    out[...] = total


def contract(place, blocks, weights, *start):
    _, depth, cols = weights.shape
    rows = blocks.shape[-1]
    return pl.pallas_call(
        contract_kernel,
        out_shape=jax.ShapeDtypeStruct((rows, cols), jnp.float32),
        in_specs=[pl.BlockSpec(memory_space=pltpu.SMEM)]
        + [pl.BlockSpec(memory_space=pltpu.VMEM)] * (2 + len(start)),
        out_specs=pl.BlockSpec(memory_space=pltpu.VMEM),
        compiler_params=LIMIT,
        cost_estimate=pl.CostEstimate(
            flops=2 * depth * rows * cols, bytes_accessed=5 * 1024 * 1024, transcendentals=0
        ),
    )(place, blocks, weights, *start)


def body(amplitudes, block_tiles, block_rows, tile_mask, block_counts):
    row_ids = block_rows[0, 0]
    slots = row_ids.shape[0]
    cols_here = tile_mask.shape[-1] * BLOCK
    rows = amplitudes.shape[0]
    blocks_here = amplitudes.shape[1] // BLOCK
    n_red = lax.axis_size("red")
    groups = server_groups()
    members = len(groups[0])
    alive = jnp.arange(slots) < block_counts[0, 0]
    here = lax.axis_index("col")
    core = here & 1
    z = here >> 1 & NZ - 1
    y = here >> 4

    halves = amplitudes.T.reshape(blocks_here, NCORE, HALF, rows)
    given = lax.ppermute(lax.dynamic_index_in_dim(halves, 1 - core, 1, False), "col", swap_pairs())
    chip = jnp.concatenate([lax.dynamic_index_in_dim(halves, core, 1, False), given])
    sources = [chip] + [lax.ppermute(chip, "col", step_pairs(s)) for s in range(1, STEPS)]

    listed = jnp.where(alive, row_ids, -1)
    other = lax.ppermute(listed, "col", swap_pairs())
    lists = jnp.where(core == 0, jnp.stack([listed, other]), jnp.stack([other, listed]))
    owners = lists >> 4
    owner_z = owners >> 1 & NZ - 1
    owner_y = owners >> 4
    server = jnp.where(core == 0, owner_z, owner_y * 2 + (owner_z & 1))
    step = jnp.where(core == 0, owner_y - y, (owner_z >> 1) - (z >> 1)) & STEPS - 1
    away = owners & 1 ^ core
    place = ((server * NCORE + jnp.arange(NCORE)[:, None]) * STEPS + step) * NCORE + away
    place = place * CAP + peer_rank(owners)
    n_places = members * NCORE * STEPS * NCORE * CAP

    flat = jnp.where(lists >= 0, place, -1).reshape(-1)
    within = ((lists & blocks_here - 1) + 1).reshape(-1)
    match = flat[None, :] == jnp.arange(n_places)[:, None]
    ask = jnp.sum(jnp.where(match, within[None, :], 0), axis=-1)
    asked = lax.all_to_all(
        ask.reshape(members, -1), "col", split_axis=0, concat_axis=0, tiled=True, axis_index_groups=groups
    )

    keep = jnp.repeat(tile_mask[0, 0] * alive[:, None], BLOCK, axis=1).astype(jnp.bfloat16)
    weights = stack(core.reshape(1), block_tiles[0, 0], keep)
    asked, weights = lax.optimization_barrier((asked, weights))
    outgoing = pick(asked.reshape(n_places), sources)
    incoming = lax.all_to_all(
        outgoing.reshape(members, -1, HALF, rows),
        "col",
        split_axis=0,
        concat_axis=0,
        tiled=True,
        axis_index_groups=groups,
    ).reshape(n_places, HALF, rows)

    place = jnp.clip(place, 0, n_places - 1)
    place_own = jnp.where(core == 0, place[0], place[1])
    place_other = jnp.where(core == 0, place[1], place[0])
    received = lax.ppermute(select(place_other, incoming), "col", swap_pairs())
    first = contract(place_own, incoming, weights)
    partial_value = contract(jnp.arange(slots, dtype=jnp.int32), received, weights, first)

    slices = partial_value.reshape(n_red, rows // n_red, cols_here)
    gathered = lax.all_to_all(slices, "red", split_axis=0, concat_axis=0, tiled=True)
    mine = jnp.sum(gathered, axis=0)
    copies = jnp.broadcast_to(mine[None], gathered.shape)
    whole = lax.all_to_all(copies, "red", split_axis=0, concat_axis=0, tiled=True)
    return whole.reshape(rows, cols_here)


def solution(mesh):
    placed = (
        P(None, ("red", "col")),
        P("red", "col", None, None),
        P("red", "col", None),
        P("red", "col", None, None),
        P("red", "col"),
    )
    return jax.shard_map(
        body, mesh=mesh, in_specs=placed, out_specs=P(None, "col"), check_vma=False
    )
```

```python
import jax
import jax.numpy as jnp
from jax import lax
from jax.experimental import pallas as pl
from jax.experimental.pallas import tpu as pltpu
from jax.sharding import PartitionSpec as P

BLOCK = 64
HALF = 32
CAP = 2
GROUP = 4
NY = 4
NZ = 8
NCORE = 2
STEPS = 4
MEMBERS = 8
LIMIT = pltpu.CompilerParams(vmem_limit_bytes=16 * 1024 * 1024)


def col_index(y, z, core):
    return (y % NY * NZ + z % NZ) * NCORE + core


def server_groups():
    along_z = [[col_index(y, z, 0) for z in range(NZ)] for y in range(NY)]
    along_y = [
        [col_index(y, 2 * pair + odd, 1) for y in range(NY) for odd in range(2)]
        for pair in range(NZ // 2)
    ]
    return along_z + along_y


def step_pairs(step):
    pairs = []
    for y in range(NY):
        for z in range(NZ):
            pairs.append((col_index(y + step, z, 0), col_index(y, z, 0)))
            pairs.append((col_index(y, z + 2 * step, 1), col_index(y, z, 1)))
    return pairs


def swap_pairs():
    return [(i, i ^ 1) for i in range(NY * NZ * NCORE)]


def front_kernel(here, count, amplitudes, rows, mine, send, note):
    core = here[0] & 1
    blocks_here = mine.shape[0]
    for pair in range(blocks_here // 2):
        width = 2 * BLOCK
        block = amplitudes[:, pl.ds(pair * width, width)].T
        for i in range(2):
            low = block[i * BLOCK : i * BLOCK + HALF]
            high = block[i * BLOCK + HALF : (i + 1) * BLOCK]
            mine[2 * pair + i] = jnp.where(core == 0, low, high)
            send[2 * pair + i] = jnp.where(core == 0, high, low)
    ids = rows[...]
    alive = lax.broadcasted_iota(jnp.int32, ids.shape, 1) < count[0]
    note[...] = jnp.zeros(note.shape, jnp.float32)
    note[0:1, : ids.shape[1]] = (ids >> 4).astype(jnp.float32)
    note[1:2, : ids.shape[1]] = jnp.where(alive, (ids & blocks_here - 1) + 1, 0).astype(jnp.float32)
    send[blocks_here] = note[...].astype(send.dtype)


def front(amplitudes, rows, count, here):
    lanes, columns = amplitudes.shape
    blocks_here = columns // BLOCK
    vmem = pl.BlockSpec(memory_space=pltpu.VMEM)
    smem = pl.BlockSpec(memory_space=pltpu.SMEM)
    return pl.pallas_call(
        front_kernel,
        out_shape=(
            jax.ShapeDtypeStruct((blocks_here, HALF, lanes), amplitudes.dtype),
            jax.ShapeDtypeStruct((blocks_here + 1, HALF, lanes), amplitudes.dtype),
        ),
        in_specs=[smem, smem, vmem, vmem],
        out_specs=(vmem, vmem),
        scratch_shapes=[pltpu.VMEM((HALF, lanes), jnp.float32)],
        compiler_params=LIMIT,
        cost_estimate=pl.CostEstimate(flops=0, bytes_accessed=4 * amplitudes.size, transcendentals=0),
    )(here, count, amplitudes, rows)


def requests_kernel(here, own, other, ask, place):
    core = here[0] & 1
    z = here[0] >> 1 & NZ - 1
    y = here[0] >> 4
    members, _, lanes = ask.shape
    per_member = NCORE * STEPS * NCORE * CAP
    square = (lanes, lanes)
    down = lax.broadcasted_iota(jnp.int32, square, 0)
    along = lax.broadcasted_iota(jnp.int32, square, 1)
    total = jnp.zeros((members, lanes), jnp.float32)
    for turn, note in enumerate((own, other)):
        device = core if turn == 0 else 1 - core
        values = note[...].astype(jnp.float32)
        owner = values[0:1].astype(jnp.int32)
        index = values[1:2]
        wide = jnp.broadcast_to(values[0:1], square)
        live = jnp.broadcast_to(index, square)
        earlier = (wide.T == wide) & (down < along) & (live.T > 0.5)
        rank = jnp.sum(jnp.where(earlier, 1.0, 0.0), axis=0, keepdims=True).astype(jnp.int32)
        owner_z = owner >> 1 & NZ - 1
        owner_y = owner >> 4
        server = jnp.where(core == 0, owner_z, owner_y * 2 + (owner_z & 1))
        step = jnp.where(core == 0, owner_y - y, (owner_z >> 1) - (z >> 1)) & STEPS - 1
        within = ((device * STEPS + step) * NCORE + (owner & 1 ^ core)) * CAP + rank
        spot = server * per_member + within
        place[turn : turn + 1, :] = jnp.minimum(spot, members * per_member - 1)
        rows = lax.broadcasted_iota(jnp.int32, (members, lanes), 0)
        asked = jnp.where(rows == server, jnp.broadcast_to(index, (members, lanes)), 0.0)
        slot = jnp.where(down == within, 1.0, 0.0)
        total += lax.dot_general(
            asked.astype(jnp.bfloat16),
            slot.astype(jnp.bfloat16),
            (((1,), (1,)), ((), ())),
            preferred_element_type=jnp.float32,
        )
    found = total.astype(jnp.int32)
    for member in range(members):
        ask[member] = jnp.broadcast_to(found[member : member + 1], ask.shape[1:])


def requests(own, other, here):
    lanes = own.shape[-1]
    vmem = pl.BlockSpec(memory_space=pltpu.VMEM)
    return pl.pallas_call(
        requests_kernel,
        out_shape=(
            jax.ShapeDtypeStruct((MEMBERS, 8, lanes), jnp.int32),
            jax.ShapeDtypeStruct((8, lanes), jnp.int32),
        ),
        in_specs=[pl.BlockSpec(memory_space=pltpu.SMEM), vmem, vmem],
        out_specs=(vmem, vmem),
        compiler_params=LIMIT,
        cost_estimate=pl.CostEstimate(flops=0, bytes_accessed=65536, transcendentals=0),
    )(here, own, other)


def stack_kernel(mine, tiles, keep, out, buf, sem):
    slots, cols = keep.shape
    chunks, _, width = buf.shape
    each = slots // chunks

    def copy(i):
        return pltpu.make_async_copy(tiles.at[:, pl.ds(i * width, width)], buf.at[i], sem.at[i])

    for i in range(chunks):
        copy(i).start()
    for i in range(chunks):
        copy(i).wait()
        for part in range(2):
            half = mine[0] if part == 0 else 1 - mine[0]
            rows = pl.ds(pl.multiple_of(half * HALF, HALF), HALF)
            for j in range(each):
                s = i * each + j
                out[part, pl.ds(s * HALF, HALF), :] = (
                    buf[i, rows, pl.ds(j * cols, cols)] * keep[pl.ds(s, 1), :]
                )


def stack(mine, tiles, keep):
    slots, cols = keep.shape
    chunks = slots // GROUP
    return pl.pallas_call(
        stack_kernel,
        out_shape=jax.ShapeDtypeStruct((2, slots * HALF, cols), tiles.dtype),
        in_specs=[
            pl.BlockSpec(memory_space=pltpu.SMEM),
            pl.BlockSpec(memory_space=pl.ANY),
            pl.BlockSpec(memory_space=pltpu.VMEM),
        ],
        out_specs=pl.BlockSpec(memory_space=pltpu.VMEM),
        scratch_shapes=[
            pltpu.VMEM((chunks, BLOCK, GROUP * cols), tiles.dtype),
            pltpu.SemaphoreType.DMA((chunks,)),
        ],
        compiler_params=LIMIT,
        cost_estimate=pl.CostEstimate(
            flops=slots * BLOCK * cols, bytes_accessed=4 * slots * BLOCK * cols, transcendentals=0
        ),
    )(mine, tiles, keep)


def pick_kernel(asked, *refs):
    *sources, out = refs
    members = asked.shape[0]
    per_member = out.shape[0] // members
    blocks_here = sources[0].shape[0] // NCORE
    for member in range(members):
        for slot in range(per_member):
            step = slot % (STEPS * NCORE * CAP) // (NCORE * CAP)
            core = slot // CAP % NCORE
            block = jnp.maximum(asked[member, 0, slot] - 1, 0)
            out[member * per_member + slot] = sources[step][core * blocks_here + block]


def pick(asked, sources):
    members = asked.shape[0]
    slots = members * NCORE * STEPS * NCORE * CAP
    shape = (slots,) + sources[0].shape[1:]
    return pl.pallas_call(
        pick_kernel,
        out_shape=jax.ShapeDtypeStruct(shape, sources[0].dtype),
        in_specs=[pl.BlockSpec(memory_space=pltpu.SMEM)]
        + [pl.BlockSpec(memory_space=pltpu.VMEM)] * len(sources),
        out_specs=pl.BlockSpec(memory_space=pltpu.VMEM),
        compiler_params=LIMIT,
        cost_estimate=pl.CostEstimate(
            flops=0, bytes_accessed=4 * slots * HALF * shape[-1], transcendentals=0
        ),
    )(asked, *sources)


def select_kernel(place, blocks, out):
    for s in range(out.shape[0]):
        out[s] = blocks[place[1, s]]


def select(place, blocks, slots):
    shape = (slots,) + blocks.shape[1:]
    return pl.pallas_call(
        select_kernel,
        out_shape=jax.ShapeDtypeStruct(shape, blocks.dtype),
        in_specs=[
            pl.BlockSpec(memory_space=pltpu.SMEM),
            pl.BlockSpec(memory_space=pltpu.VMEM),
        ],
        out_specs=pl.BlockSpec(memory_space=pltpu.VMEM),
        compiler_params=LIMIT,
        cost_estimate=pl.CostEstimate(
            flops=0, bytes_accessed=2 * blocks.size, transcendentals=0
        ),
    )(place, blocks)


def contract_kernel(place, blocks, weights, *refs):
    *start, out = refs
    total = start[0][...] if start else jnp.zeros(out.shape, jnp.float32)
    half = 1 if start else 0
    at = (lambda i: i) if start else (lambda i: place[0, i])
    each = 2 * GROUP
    depth = each * HALF
    for g in range(weights.shape[1] // depth):
        lhs = jnp.concatenate([blocks[at(g * each + s)] for s in range(each)], axis=0)
        total += lax.dot_general(
            lhs,
            weights[half, pl.ds(g * depth, depth), :],
            (((0,), (0,)), ((), ())),
            preferred_element_type=jnp.float32,
        )
    out[...] = total


def contract(place, blocks, weights, *start):
    _, depth, cols = weights.shape
    rows = blocks.shape[-1]
    return pl.pallas_call(
        contract_kernel,
        out_shape=jax.ShapeDtypeStruct((rows, cols), jnp.float32),
        in_specs=[pl.BlockSpec(memory_space=pltpu.SMEM)]
        + [pl.BlockSpec(memory_space=pltpu.VMEM)] * (2 + len(start)),
        out_specs=pl.BlockSpec(memory_space=pltpu.VMEM),
        compiler_params=LIMIT,
        cost_estimate=pl.CostEstimate(
            flops=2 * depth * rows * cols, bytes_accessed=5 * 1024 * 1024, transcendentals=0
        ),
    )(place, blocks, weights, *start)


def body(amplitudes, block_tiles, block_rows, tile_mask, block_counts):
    slots = block_rows.shape[-1]
    cols_here = tile_mask.shape[-1] * BLOCK
    rows = amplitudes.shape[0]
    n_red = lax.axis_size("red")
    groups = server_groups()
    here = lax.axis_index("col").astype(jnp.int32)
    core = here & 1
    here = here.reshape(1)

    mine, send = front(amplitudes, block_rows[0], block_counts[0], here)
    given = lax.ppermute(send, "col", swap_pairs())
    chip = jnp.concatenate([mine, given[:-1]])
    sources = [chip] + [lax.ppermute(chip, "col", step_pairs(s)) for s in range(1, STEPS)]

    ask, place = requests(send[-1], given[-1], here)
    asked = lax.all_to_all(
        ask, "col", split_axis=0, concat_axis=0, tiled=True, axis_index_groups=groups
    )

    alive = jnp.arange(slots) < block_counts[0, 0]
    keep = jnp.repeat(tile_mask[0, 0] * alive[:, None], BLOCK, axis=1).astype(jnp.bfloat16)
    weights = stack(core.reshape(1), block_tiles[0, 0], keep)
    asked, weights = lax.optimization_barrier((asked, weights))
    outgoing = pick(asked, sources)
    incoming = lax.all_to_all(
        outgoing.reshape(MEMBERS, -1, HALF, rows),
        "col",
        split_axis=0,
        concat_axis=0,
        tiled=True,
        axis_index_groups=groups,
    ).reshape(-1, HALF, rows)

    received = lax.ppermute(select(place, incoming, slots), "col", swap_pairs())
    first = contract(place, incoming, weights)
    partial_value = contract(place, received, weights, first)

    slices = partial_value.reshape(n_red, rows // n_red, cols_here)
    gathered = lax.all_to_all(slices, "red", split_axis=0, concat_axis=0, tiled=True)
    mine = jnp.sum(gathered, axis=0)
    copies = jnp.broadcast_to(mine[None], gathered.shape)
    whole = lax.all_to_all(copies, "red", split_axis=0, concat_axis=0, tiled=True)
    return whole.reshape(rows, cols_here)


def solution(mesh):
    placed = (
        P(None, ("red", "col")),
        P("red", "col", None, None),
        P("red", "col", None),
        P("red", "col", None, None),
        P("red", "col"),
    )
    return jax.shard_map(
        body, mesh=mesh, in_specs=placed, out_specs=P(None, "col"), check_vma=False
    )
```

```python
import jax
import jax.numpy as jnp
from jax import lax
from jax.experimental import pallas as pl
from jax.experimental.pallas import tpu as pltpu
from jax.sharding import PartitionSpec as P

BLOCK = 64
HALF = 32
CAP = 2
GROUP = 4
NY = 4
NZ = 8
NCORE = 2
STEPS = 4
MEMBERS = 8
LIMIT = pltpu.CompilerParams(vmem_limit_bytes=16 * 1024 * 1024)


def col_index(y, z, core):
    return (y % NY * NZ + z % NZ) * NCORE + core


def server_groups():
    along_z = [[col_index(y, z, 0) for z in range(NZ)] for y in range(NY)]
    along_y = [
        [col_index(y, 2 * pair + odd, 1) for y in range(NY) for odd in range(2)]
        for pair in range(NZ // 2)
    ]
    return along_z + along_y


def step_pairs(step):
    pairs = []
    for y in range(NY):
        for z in range(NZ):
            pairs.append((col_index(y + step, z, 0), col_index(y, z, 0)))
            pairs.append((col_index(y, z + 2 * step, 1), col_index(y, z, 1)))
    return pairs


def swap_pairs():
    return [(i, i ^ 1) for i in range(NY * NZ * NCORE)]


def front_kernel(here, count, amplitudes, rows, mine, send, listed, buf, ids_buf, note, sem):
    core = here[0] & 1
    blocks_here = mine.shape[0]
    pairs, _, width = buf.shape
    ids_copy = pltpu.make_async_copy(rows, ids_buf, sem.at[pairs])
    ids_copy.start()

    def copy(pair):
        part = amplitudes.at[:, pl.ds(pair * width, width)]
        return pltpu.make_async_copy(part, buf.at[pair], sem.at[pair])

    for pair in range(pairs):
        copy(pair).start()
    for pair in range(pairs):
        copy(pair).wait()
        block = buf[pair].T
        for i in range(2):
            low = block[i * BLOCK : i * BLOCK + HALF]
            high = block[i * BLOCK + HALF : (i + 1) * BLOCK]
            mine[2 * pair + i] = jnp.where(core == 0, low, high)
            send[2 * pair + i] = jnp.where(core == 0, high, low)
    ids_copy.wait()
    ids = ids_buf[...]
    alive = lax.broadcasted_iota(jnp.int32, ids.shape, 1) < count[0]
    note[...] = jnp.zeros(note.shape, jnp.float32)
    note[0:1, : ids.shape[1]] = (ids >> 4).astype(jnp.float32)
    note[1:2, : ids.shape[1]] = jnp.where(alive, (ids & blocks_here - 1) + 1, 0).astype(jnp.float32)
    listed[...] = note[...].astype(listed.dtype)
    send[blocks_here] = note[...].astype(send.dtype)


def front(amplitudes, rows, count, here):
    lanes, columns = amplitudes.shape
    blocks_here = columns // BLOCK
    pairs = blocks_here // 2
    vmem = pl.BlockSpec(memory_space=pltpu.VMEM)
    smem = pl.BlockSpec(memory_space=pltpu.SMEM)
    hbm = pl.BlockSpec(memory_space=pltpu.HBM)
    return pl.pallas_call(
        front_kernel,
        out_shape=(
            jax.ShapeDtypeStruct((blocks_here, HALF, lanes), amplitudes.dtype),
            jax.ShapeDtypeStruct((blocks_here + 1, HALF, lanes), amplitudes.dtype),
            jax.ShapeDtypeStruct((HALF, lanes), amplitudes.dtype),
        ),
        in_specs=[smem, smem, hbm, hbm],
        out_specs=(vmem, vmem, vmem),
        scratch_shapes=[
            pltpu.VMEM((pairs, lanes, 2 * BLOCK), amplitudes.dtype),
            pltpu.VMEM(rows.shape, rows.dtype),
            pltpu.VMEM((HALF, lanes), jnp.float32),
            pltpu.SemaphoreType.DMA((pairs + 1,)),
        ],
        compiler_params=pltpu.CompilerParams(vmem_limit_bytes=60 * 1024 * 1024),
        cost_estimate=pl.CostEstimate(flops=0, bytes_accessed=4 * amplitudes.size, transcendentals=0),
    )(here, count, amplitudes, rows)


def requests_kernel(here, own, other, ask, place):
    core = here[0] & 1
    z = here[0] >> 1 & NZ - 1
    y = here[0] >> 4
    members, _, lanes = ask.shape
    per_member = NCORE * STEPS * NCORE * CAP
    square = (lanes, lanes)
    down = lax.broadcasted_iota(jnp.int32, square, 0)
    along = lax.broadcasted_iota(jnp.int32, square, 1)
    total = jnp.zeros((members, lanes), jnp.float32)
    for turn, note in enumerate((own[...], other[other.shape[0] - 1])):
        device = core if turn == 0 else 1 - core
        values = note.astype(jnp.float32)
        owner = values[0:1].astype(jnp.int32)
        index = values[1:2]
        wide = jnp.broadcast_to(values[0:1], square)
        live = jnp.broadcast_to(index, square)
        earlier = (wide.T == wide) & (down < along) & (live.T > 0.5)
        rank = jnp.sum(jnp.where(earlier, 1.0, 0.0), axis=0, keepdims=True).astype(jnp.int32)
        owner_z = owner >> 1 & NZ - 1
        owner_y = owner >> 4
        server = jnp.where(core == 0, owner_z, owner_y * 2 + (owner_z & 1))
        step = jnp.where(core == 0, owner_y - y, (owner_z >> 1) - (z >> 1)) & STEPS - 1
        within = ((device * STEPS + step) * NCORE + (owner & 1 ^ core)) * CAP + rank
        spot = server * per_member + within
        place[turn : turn + 1, :] = jnp.minimum(spot, members * per_member - 1)
        rows = lax.broadcasted_iota(jnp.int32, (members, lanes), 0)
        asked = jnp.where(rows == server, jnp.broadcast_to(index, (members, lanes)), 0.0)
        slot = jnp.where(down == within, 1.0, 0.0)
        total += lax.dot_general(
            asked.astype(jnp.bfloat16),
            slot.astype(jnp.bfloat16),
            (((1,), (1,)), ((), ())),
            preferred_element_type=jnp.float32,
        )
    found = total.astype(jnp.int32)
    for member in range(members):
        ask[member] = jnp.broadcast_to(found[member : member + 1], ask.shape[1:])


def requests(own, other, here):
    lanes = own.shape[-1]
    vmem = pl.BlockSpec(memory_space=pltpu.VMEM)
    return pl.pallas_call(
        requests_kernel,
        out_shape=(
            jax.ShapeDtypeStruct((MEMBERS, 8, lanes), jnp.int32),
            jax.ShapeDtypeStruct((8, lanes), jnp.int32),
        ),
        in_specs=[pl.BlockSpec(memory_space=pltpu.SMEM), vmem, vmem],
        out_specs=(vmem, vmem),
        compiler_params=LIMIT,
        cost_estimate=pl.CostEstimate(flops=0, bytes_accessed=65536, transcendentals=0),
    )(here, own, other)


def stack_kernel(mine, tiles, keep, out, buf, sem):
    slots, cols = keep.shape
    chunks, _, width = buf.shape
    each = slots // chunks

    def copy(i):
        return pltpu.make_async_copy(tiles.at[:, pl.ds(i * width, width)], buf.at[i], sem.at[i])

    for i in range(chunks):
        copy(i).start()
    for i in range(chunks):
        copy(i).wait()
        for part in range(2):
            half = mine[0] if part == 0 else 1 - mine[0]
            rows = pl.ds(pl.multiple_of(half * HALF, HALF), HALF)
            for j in range(each):
                s = i * each + j
                out[part, pl.ds(s * HALF, HALF), :] = (
                    buf[i, rows, pl.ds(j * cols, cols)] * keep[pl.ds(s, 1), :]
                )


def stack(mine, tiles, keep):
    slots, cols = keep.shape
    chunks = slots // GROUP
    return pl.pallas_call(
        stack_kernel,
        out_shape=jax.ShapeDtypeStruct((2, slots * HALF, cols), tiles.dtype),
        in_specs=[
            pl.BlockSpec(memory_space=pltpu.SMEM),
            pl.BlockSpec(memory_space=pl.ANY),
            pl.BlockSpec(memory_space=pltpu.VMEM),
        ],
        out_specs=pl.BlockSpec(memory_space=pltpu.VMEM),
        scratch_shapes=[
            pltpu.VMEM((chunks, BLOCK, GROUP * cols), tiles.dtype),
            pltpu.SemaphoreType.DMA((chunks,)),
        ],
        compiler_params=LIMIT,
        cost_estimate=pl.CostEstimate(
            flops=slots * BLOCK * cols, bytes_accessed=4 * slots * BLOCK * cols, transcendentals=0
        ),
    )(mine, tiles, keep)


def pick_kernel(asked, *refs):
    *sources, out = refs
    members = asked.shape[0]
    per_member = out.shape[0] // members
    blocks_here = sources[0].shape[0] // NCORE
    for member in range(members):
        for slot in range(per_member):
            step = slot % (STEPS * NCORE * CAP) // (NCORE * CAP)
            core = slot // CAP % NCORE
            block = jnp.maximum(asked[member, 0, slot] - 1, 0)
            out[member * per_member + slot] = sources[step][core * blocks_here + block]


def pick(asked, sources):
    members = asked.shape[0]
    slots = members * NCORE * STEPS * NCORE * CAP
    shape = (slots,) + sources[0].shape[1:]
    return pl.pallas_call(
        pick_kernel,
        out_shape=jax.ShapeDtypeStruct(shape, sources[0].dtype),
        in_specs=[pl.BlockSpec(memory_space=pltpu.SMEM)]
        + [pl.BlockSpec(memory_space=pltpu.VMEM)] * len(sources),
        out_specs=pl.BlockSpec(memory_space=pltpu.VMEM),
        compiler_params=LIMIT,
        cost_estimate=pl.CostEstimate(
            flops=0, bytes_accessed=4 * slots * HALF * shape[-1], transcendentals=0
        ),
    )(asked, *sources)


def contract_half(blocks, weights, half, total):
    each = 2 * GROUP
    depth = each * HALF
    for g in range(weights.shape[1] // depth):
        lhs = jnp.concatenate([blocks(g * each + s) for s in range(each)], axis=0)
        total += lax.dot_general(
            lhs,
            weights[half, pl.ds(g * depth, depth), :],
            (((0,), (0,)), ((), ())),
            preferred_element_type=jnp.float32,
        )
    return total


def first_kernel(place, blocks, weights, chosen, out):
    for s in range(chosen.shape[0]):
        chosen[s] = blocks[place[1, s]]
    out[...] = contract_half(
        lambda s: blocks[place[0, s]], weights, 0, jnp.zeros(out.shape, jnp.float32)
    )


def second_kernel(blocks, weights, start, out):
    out[...] = contract_half(lambda s: blocks[s], weights, 1, start[...])


def first(place, blocks, weights):
    _, depth, cols = weights.shape
    half, rows = blocks.shape[1:]
    vmem = pl.BlockSpec(memory_space=pltpu.VMEM)
    return pl.pallas_call(
        first_kernel,
        out_shape=(
            jax.ShapeDtypeStruct((depth // half, half, rows), blocks.dtype),
            jax.ShapeDtypeStruct((rows, cols), jnp.float32),
        ),
        in_specs=[pl.BlockSpec(memory_space=pltpu.SMEM), vmem, vmem],
        out_specs=(vmem, vmem),
        compiler_params=LIMIT,
        cost_estimate=pl.CostEstimate(
            flops=2 * depth * rows * cols, bytes_accessed=4 * 1024 * 1024, transcendentals=0
        ),
    )(place, blocks, weights)


def second(blocks, weights, start):
    _, depth, cols = weights.shape
    vmem = pl.BlockSpec(memory_space=pltpu.VMEM)
    return pl.pallas_call(
        second_kernel,
        out_shape=jax.ShapeDtypeStruct(start.shape, start.dtype),
        in_specs=[vmem, vmem, vmem],
        out_specs=vmem,
        compiler_params=LIMIT,
        cost_estimate=pl.CostEstimate(
            flops=2 * depth * start.size, bytes_accessed=2 * 1024 * 1024, transcendentals=0
        ),
    )(blocks, weights, start)


def body(amplitudes, block_tiles, block_rows, tile_mask, block_counts):
    slots = block_rows.shape[-1]
    cols_here = tile_mask.shape[-1] * BLOCK
    rows = amplitudes.shape[0]
    n_red = lax.axis_size("red")
    groups = server_groups()
    here = lax.axis_index("col").astype(jnp.int32)
    core = here & 1
    here = here.reshape(1)

    mine, send, listed = front(amplitudes, block_rows[0], block_counts[0], here)
    given = lax.ppermute(send, "col", swap_pairs())
    chip = jnp.concatenate([mine, given])
    sources = [chip] + [lax.ppermute(chip, "col", step_pairs(s)) for s in range(1, STEPS)]

    ask, place = requests(listed, given, here)
    asked = lax.all_to_all(
        ask, "col", split_axis=0, concat_axis=0, tiled=True, axis_index_groups=groups
    )

    alive = jnp.arange(slots) < block_counts[0, 0]
    keep = jnp.repeat(tile_mask[0, 0] * alive[:, None], BLOCK, axis=1).astype(jnp.bfloat16)
    weights = stack(core.reshape(1), block_tiles[0, 0], keep)
    asked, weights = lax.optimization_barrier((asked, weights))
    outgoing = pick(asked, sources)
    incoming = lax.all_to_all(
        outgoing.reshape(MEMBERS, -1, HALF, rows),
        "col",
        split_axis=0,
        concat_axis=0,
        tiled=True,
        axis_index_groups=groups,
    ).reshape(-1, HALF, rows)

    chosen, product = first(place, incoming, weights)
    received = lax.ppermute(chosen, "col", swap_pairs())
    partial_value = second(received, weights, product)

    slices = partial_value.reshape(n_red, rows // n_red, cols_here)
    gathered = lax.all_to_all(slices, "red", split_axis=0, concat_axis=0, tiled=True)
    mine = jnp.sum(gathered, axis=0)
    copies = jnp.broadcast_to(mine[None], gathered.shape)
    whole = lax.all_to_all(copies, "red", split_axis=0, concat_axis=0, tiled=True)
    return whole.reshape(rows, cols_here)


def solution(mesh):
    placed = (
        P(None, ("red", "col")),
        P("red", "col", None, None),
        P("red", "col", None),
        P("red", "col", None, None),
        P("red", "col"),
    )
    return jax.shard_map(
        body, mesh=mesh, in_specs=placed, out_specs=P(None, "col"), check_vma=False
    )
```

```python
import jax
import jax.numpy as jnp
from jax import lax
from jax.experimental import pallas as pl
from jax.experimental.pallas import tpu as pltpu
from jax.sharding import PartitionSpec as P

BLOCK = 64
CAP = 2
GROUP = 4
NY = 4
NZ = 8
NCORE = 2
STEPS = 4
MEMBERS = 8
LIMIT = pltpu.CompilerParams(vmem_limit_bytes=16 * 1024 * 1024)


def col_index(y, z, core):
    return (y % NY * NZ + z % NZ) * NCORE + core


def server_groups():
    along_z = [[col_index(y, z, 0) for z in range(NZ)] for y in range(NY)]
    along_y = [
        [col_index(y, 2 * pair + odd, 1) for y in range(NY) for odd in range(2)]
        for pair in range(NZ // 2)
    ]
    return along_z + along_y


def step_pairs(step):
    pairs = []
    for y in range(NY):
        for z in range(NZ):
            pairs.append((col_index(y + step, z, 0), col_index(y, z, 0)))
            pairs.append((col_index(y, z + 2 * step, 1), col_index(y, z, 1)))
    return pairs


def swap_pairs():
    return [(i, i ^ 1) for i in range(NY * NZ * NCORE)]


def requests_kernel(here, count, rows, ask, place):
    core = here[0] & 1
    z = here[0] >> 1 & NZ - 1
    y = here[0] >> 4
    members, _, lanes = ask.shape
    slots = rows.shape[1]
    per_member = STEPS * NCORE * CAP
    square = (lanes, lanes)
    down = lax.broadcasted_iota(jnp.int32, square, 0)
    along = lax.broadcasted_iota(jnp.int32, square, 1)
    place[...] = jnp.zeros(place.shape, jnp.int32)
    place[0:1, :slots] = rows[...]
    ids = place[0:1, :]
    live = along < jnp.minimum(count[0], slots)
    owner = ids >> 4
    index = jnp.where(live[0:1], (ids & 15) + 1, 0).astype(jnp.float32)
    wide = jnp.broadcast_to(owner.astype(jnp.float32), square)
    earlier = (wide.T == wide) & (down < along) & (down < jnp.minimum(count[0], slots))
    rank = jnp.sum(jnp.where(earlier, 1.0, 0.0), axis=0, keepdims=True).astype(jnp.int32)
    owner_z = owner >> 1 & NZ - 1
    owner_y = owner >> 4
    server = jnp.where(core == 0, owner_z, owner_y * 2 + (owner_z & 1))
    step = jnp.where(core == 0, owner_y - y, (owner_z >> 1) - (z >> 1)) & STEPS - 1
    within = (step * NCORE + (owner & 1 ^ core)) * CAP + rank
    place[0:1, :] = jnp.minimum(server * per_member + within, members * per_member - 1)
    line = lax.broadcasted_iota(jnp.int32, (members, lanes), 0)
    asked = jnp.where(line == server, jnp.broadcast_to(index, (members, lanes)), 0.0)
    slot = jnp.where(down == within, 1.0, 0.0)
    found = lax.dot_general(
        asked.astype(jnp.bfloat16),
        slot.astype(jnp.bfloat16),
        (((1,), (1,)), ((), ())),
        preferred_element_type=jnp.float32,
    ).astype(jnp.int32)
    for member in range(members):
        ask[member] = jnp.broadcast_to(found[member : member + 1], ask.shape[1:])


def requests(here, count, rows):
    lanes = 128
    vmem = pl.BlockSpec(memory_space=pltpu.VMEM)
    smem = pl.BlockSpec(memory_space=pltpu.SMEM)
    return pl.pallas_call(
        requests_kernel,
        out_shape=(
            jax.ShapeDtypeStruct((MEMBERS, 8, lanes), jnp.int32),
            jax.ShapeDtypeStruct((8, lanes), jnp.int32),
        ),
        in_specs=[smem, smem, vmem],
        out_specs=(vmem, vmem),
        compiler_params=LIMIT,
        cost_estimate=pl.CostEstimate(flops=0, bytes_accessed=65536, transcendentals=0),
    )(here, count, rows)


def stack_kernel(tiles, keep, out, buf, sem):
    slots, cols = keep.shape
    chunks, _, width = buf.shape
    each = slots // chunks

    def copy(i):
        return pltpu.make_async_copy(tiles.at[:, pl.ds(i * width, width)], buf.at[i], sem.at[i])

    for i in range(chunks):
        copy(i).start()
    for i in range(chunks):
        copy(i).wait()
        for j in range(each):
            s = i * each + j
            out[pl.ds(s * BLOCK, BLOCK), :] = buf[i, :, pl.ds(j * cols, cols)] * keep[pl.ds(s, 1), :]


def stack(tiles, keep):
    slots, cols = keep.shape
    chunks = slots // GROUP
    return pl.pallas_call(
        stack_kernel,
        out_shape=jax.ShapeDtypeStruct((slots * BLOCK, cols), tiles.dtype),
        in_specs=[
            pl.BlockSpec(memory_space=pl.ANY),
            pl.BlockSpec(memory_space=pltpu.VMEM),
        ],
        out_specs=pl.BlockSpec(memory_space=pltpu.VMEM),
        scratch_shapes=[
            pltpu.VMEM((chunks, BLOCK, GROUP * cols), tiles.dtype),
            pltpu.SemaphoreType.DMA((chunks,)),
        ],
        compiler_params=LIMIT,
        cost_estimate=pl.CostEstimate(
            flops=slots * BLOCK * cols, bytes_accessed=4 * slots * BLOCK * cols, transcendentals=0
        ),
    )(tiles, keep)


def pick_kernel(asked, *refs):
    *sources, out = refs
    members = asked.shape[0]
    per_member = out.shape[0] // members
    blocks_here = sources[0].shape[0] // NCORE
    for member in range(members):
        for slot in range(per_member):
            step = slot // (NCORE * CAP)
            core = slot // CAP % NCORE
            block = jnp.maximum(asked[member, 0, slot] - 1, 0)
            out[member * per_member + slot] = sources[step][core * blocks_here + block]


def pick(asked, sources):
    members = asked.shape[0]
    slots = members * STEPS * NCORE * CAP
    shape = (slots,) + sources[0].shape[1:]
    return pl.pallas_call(
        pick_kernel,
        out_shape=jax.ShapeDtypeStruct(shape, sources[0].dtype),
        in_specs=[pl.BlockSpec(memory_space=pltpu.SMEM)]
        + [pl.BlockSpec(memory_space=pltpu.VMEM)] * len(sources),
        out_specs=pl.BlockSpec(memory_space=pltpu.VMEM),
        compiler_params=LIMIT,
        cost_estimate=pl.CostEstimate(
            flops=0, bytes_accessed=4 * slots * BLOCK * shape[-1], transcendentals=0
        ),
    )(asked, *sources)


def contract_kernel(place, blocks, weights, out):
    total = jnp.zeros(out.shape, jnp.float32)
    depth = GROUP * BLOCK
    for g in range(weights.shape[0] // depth):
        lhs = jnp.concatenate([blocks[place[0, g * GROUP + s]] for s in range(GROUP)], axis=0)
        total += lax.dot_general(
            lhs,
            weights[pl.ds(g * depth, depth), :],
            (((0,), (0,)), ((), ())),
            preferred_element_type=jnp.float32,
        )
    out[...] = total


def contract(place, blocks, weights):
    depth, cols = weights.shape
    rows = blocks.shape[-1]
    return pl.pallas_call(
        contract_kernel,
        out_shape=jax.ShapeDtypeStruct((rows, cols), jnp.float32),
        in_specs=[
            pl.BlockSpec(memory_space=pltpu.SMEM),
            pl.BlockSpec(memory_space=pltpu.VMEM),
            pl.BlockSpec(memory_space=pltpu.VMEM),
        ],
        out_specs=pl.BlockSpec(memory_space=pltpu.VMEM),
        compiler_params=LIMIT,
        cost_estimate=pl.CostEstimate(
            flops=2 * depth * rows * cols, bytes_accessed=5 * 1024 * 1024, transcendentals=0
        ),
    )(place, blocks, weights)


def body(amplitudes, block_tiles, block_rows, tile_mask, block_counts):
    slots = block_rows.shape[-1]
    cols_here = tile_mask.shape[-1] * BLOCK
    rows = amplitudes.shape[0]
    n_red = lax.axis_size("red")
    groups = server_groups()
    here = lax.axis_index("col").astype(jnp.int32).reshape(1)

    own = amplitudes.T.reshape(-1, BLOCK, rows)
    chip = jnp.concatenate([own, lax.ppermute(own, "col", swap_pairs())])
    sources = [chip] + [lax.ppermute(chip, "col", step_pairs(s)) for s in range(1, STEPS)]

    ask, place = requests(here, block_counts[0], block_rows[0])
    asked = lax.all_to_all(
        ask, "col", split_axis=0, concat_axis=0, tiled=True, axis_index_groups=groups
    )

    alive = jnp.arange(slots) < block_counts[0, 0]
    keep = jnp.repeat(tile_mask[0, 0] * alive[:, None], BLOCK, axis=1).astype(jnp.bfloat16)
    weights = stack(block_tiles[0, 0], keep)
    asked, weights = lax.optimization_barrier((asked, weights))
    outgoing = pick(asked, sources)
    incoming = lax.all_to_all(
        outgoing.reshape(MEMBERS, -1, BLOCK, rows),
        "col",
        split_axis=0,
        concat_axis=0,
        tiled=True,
        axis_index_groups=groups,
    ).reshape(-1, BLOCK, rows)
    partial_value = contract(place, incoming, weights)

    slices = partial_value.reshape(n_red, rows // n_red, cols_here)
    gathered = lax.all_to_all(slices, "red", split_axis=0, concat_axis=0, tiled=True)
    mine = jnp.sum(gathered, axis=0)
    copies = jnp.broadcast_to(mine[None], gathered.shape)
    whole = lax.all_to_all(copies, "red", split_axis=0, concat_axis=0, tiled=True)
    return whole.reshape(rows, cols_here)


def solution(mesh):
    placed = (
        P(None, ("red", "col")),
        P("red", "col", None, None),
        P("red", "col", None),
        P("red", "col", None, None),
        P("red", "col"),
    )
    return jax.shard_map(
        body, mesh=mesh, in_specs=placed, out_specs=P(None, "col"), check_vma=False
    )
```

```python
import jax
import jax.numpy as jnp
from jax import lax
from jax.experimental import pallas as pl
from jax.experimental.pallas import tpu as pltpu
from jax.sharding import PartitionSpec as P

BLOCK = 64
HALF = 32
CAP = 2
GROUP = 4
NY = 4
NZ = 8
NCORE = 2
STEPS = 4
MEMBERS = 8
LIMIT = pltpu.CompilerParams(vmem_limit_bytes=16 * 1024 * 1024)


def col_index(y, z, core):
    return (y % NY * NZ + z % NZ) * NCORE + core


def server_groups():
    along_z = [[col_index(y, z, 0) for z in range(NZ)] for y in range(NY)]
    along_y = [
        [col_index(y, 2 * pair + odd, 1) for y in range(NY) for odd in range(2)]
        for pair in range(NZ // 2)
    ]
    return along_z + along_y


def step_pairs(step):
    pairs = []
    for y in range(NY):
        for z in range(NZ):
            pairs.append((col_index(y + step, z, 0), col_index(y, z, 0)))
            pairs.append((col_index(y, z + 2 * step, 1), col_index(y, z, 1)))
    return pairs


def swap_pairs():
    return [(i, i ^ 1) for i in range(NY * NZ * NCORE)]


def front_kernel(here, count, amplitudes, rows, mine, send, note):
    core = here[0] & 1
    blocks_here = mine.shape[0]
    for pair in range(blocks_here // 2):
        width = 2 * BLOCK
        block = amplitudes[:, pl.ds(pair * width, width)].T
        for i in range(2):
            low = block[i * BLOCK : i * BLOCK + HALF]
            high = block[i * BLOCK + HALF : (i + 1) * BLOCK]
            mine[2 * pair + i] = jnp.where(core == 0, low, high)
            send[2 * pair + i] = jnp.where(core == 0, high, low)
    ids = rows[...]
    alive = lax.broadcasted_iota(jnp.int32, ids.shape, 1) < count[0]
    note[...] = jnp.zeros(note.shape, jnp.float32)
    note[0:1, : ids.shape[1]] = (ids >> 4).astype(jnp.float32)
    note[1:2, : ids.shape[1]] = jnp.where(alive, (ids & blocks_here - 1) + 1, 0).astype(jnp.float32)
    send[blocks_here] = note[...].astype(send.dtype)


def front(amplitudes, rows, count, here):
    lanes, columns = amplitudes.shape
    blocks_here = columns // BLOCK
    vmem = pl.BlockSpec(memory_space=pltpu.VMEM)
    smem = pl.BlockSpec(memory_space=pltpu.SMEM)
    return pl.pallas_call(
        front_kernel,
        out_shape=(
            jax.ShapeDtypeStruct((blocks_here, HALF, lanes), amplitudes.dtype),
            jax.ShapeDtypeStruct((blocks_here + 1, HALF, lanes), amplitudes.dtype),
        ),
        in_specs=[smem, smem, vmem, vmem],
        out_specs=(vmem, vmem),
        scratch_shapes=[pltpu.VMEM((HALF, lanes), jnp.float32)],
        compiler_params=LIMIT,
        cost_estimate=pl.CostEstimate(flops=0, bytes_accessed=4 * amplitudes.size, transcendentals=0),
    )(here, count, amplitudes, rows)


def requests_kernel(here, own, other, ask, place):
    core = here[0] & 1
    z = here[0] >> 1 & NZ - 1
    y = here[0] >> 4
    members, _, lanes = ask.shape
    per_member = NCORE * STEPS * NCORE * CAP
    square = (lanes, lanes)
    down = lax.broadcasted_iota(jnp.int32, square, 0)
    along = lax.broadcasted_iota(jnp.int32, square, 1)
    total = jnp.zeros((members, lanes), jnp.float32)
    for turn, note in enumerate((own[...], other[other.shape[0] - 1])):
        device = core if turn == 0 else 1 - core
        values = note.astype(jnp.float32)
        owner = values[0:1].astype(jnp.int32)
        index = values[1:2]
        wide = jnp.broadcast_to(values[0:1], square)
        live = jnp.broadcast_to(index, square)
        earlier = (wide.T == wide) & (down < along) & (live.T > 0.5)
        rank = jnp.sum(jnp.where(earlier, 1.0, 0.0), axis=0, keepdims=True).astype(jnp.int32)
        owner_z = owner >> 1 & NZ - 1
        owner_y = owner >> 4
        server = jnp.where(core == 0, owner_z, owner_y * 2 + (owner_z & 1))
        step = jnp.where(core == 0, owner_y - y, (owner_z >> 1) - (z >> 1)) & STEPS - 1
        within = ((device * STEPS + step) * NCORE + (owner & 1 ^ core)) * CAP + rank
        spot = server * per_member + within
        place[turn : turn + 1, :] = jnp.minimum(spot, members * per_member - 1)
        rows = lax.broadcasted_iota(jnp.int32, (members, lanes), 0)
        asked = jnp.where(rows == server, jnp.broadcast_to(index, (members, lanes)), 0.0)
        slot = jnp.where(down == within, 1.0, 0.0)
        total += lax.dot_general(
            asked.astype(jnp.bfloat16),
            slot.astype(jnp.bfloat16),
            (((1,), (1,)), ((), ())),
            preferred_element_type=jnp.float32,
        )
    found = total.astype(jnp.int32)
    for member in range(members):
        ask[member] = jnp.broadcast_to(found[member : member + 1], ask.shape[1:])


def requests(own, other, here):
    lanes = own.shape[-1]
    vmem = pl.BlockSpec(memory_space=pltpu.VMEM)
    return pl.pallas_call(
        requests_kernel,
        out_shape=(
            jax.ShapeDtypeStruct((MEMBERS, 8, lanes), jnp.int32),
            jax.ShapeDtypeStruct((8, lanes), jnp.int32),
        ),
        in_specs=[pl.BlockSpec(memory_space=pltpu.SMEM), vmem, vmem],
        out_specs=(vmem, vmem),
        compiler_params=LIMIT,
        cost_estimate=pl.CostEstimate(flops=0, bytes_accessed=65536, transcendentals=0),
    )(here, own, other)


def stack_kernel(mine, tiles, keep, out, buf, sem):
    slots, cols = keep.shape
    chunks, _, width = buf.shape
    each = slots // chunks

    def copy(i):
        return pltpu.make_async_copy(tiles.at[:, pl.ds(i * width, width)], buf.at[i], sem.at[i])

    for i in range(chunks):
        copy(i).start()
    for i in range(chunks):
        copy(i).wait()
        for part in range(2):
            half = mine[0] if part == 0 else 1 - mine[0]
            rows = pl.ds(pl.multiple_of(half * HALF, HALF), HALF)
            for j in range(each):
                s = i * each + j
                out[part, pl.ds(s * HALF, HALF), :] = (
                    buf[i, rows, pl.ds(j * cols, cols)] * keep[pl.ds(s, 1), :]
                )


def stack(mine, tiles, keep):
    slots, cols = keep.shape
    chunks = slots // GROUP
    return pl.pallas_call(
        stack_kernel,
        out_shape=jax.ShapeDtypeStruct((2, slots * HALF, cols), tiles.dtype),
        in_specs=[
            pl.BlockSpec(memory_space=pltpu.SMEM),
            pl.BlockSpec(memory_space=pl.ANY),
            pl.BlockSpec(memory_space=pltpu.VMEM),
        ],
        out_specs=pl.BlockSpec(memory_space=pltpu.VMEM),
        scratch_shapes=[
            pltpu.VMEM((chunks, BLOCK, GROUP * cols), tiles.dtype),
            pltpu.SemaphoreType.DMA((chunks,)),
        ],
        compiler_params=LIMIT,
        cost_estimate=pl.CostEstimate(
            flops=slots * BLOCK * cols, bytes_accessed=4 * slots * BLOCK * cols, transcendentals=0
        ),
    )(mine, tiles, keep)


def pick_kernel(asked, *refs):
    *sources, out = refs
    members = asked.shape[0]
    per_member = out.shape[0] // members
    blocks_here = sources[0].shape[0] // NCORE
    for member in range(members):
        for slot in range(per_member):
            step = slot % (STEPS * NCORE * CAP) // (NCORE * CAP)
            core = slot // CAP % NCORE
            block = jnp.maximum(asked[member, 0, slot] - 1, 0)
            out[member * per_member + slot] = sources[step][core * blocks_here + block]


def pick(asked, sources):
    members = asked.shape[0]
    slots = members * NCORE * STEPS * NCORE * CAP
    shape = (slots,) + sources[0].shape[1:]
    return pl.pallas_call(
        pick_kernel,
        out_shape=jax.ShapeDtypeStruct(shape, sources[0].dtype),
        in_specs=[pl.BlockSpec(memory_space=pltpu.SMEM)]
        + [pl.BlockSpec(memory_space=pltpu.VMEM)] * len(sources),
        out_specs=pl.BlockSpec(memory_space=pltpu.VMEM),
        compiler_params=LIMIT,
        cost_estimate=pl.CostEstimate(
            flops=0, bytes_accessed=4 * slots * HALF * shape[-1], transcendentals=0
        ),
    )(asked, *sources)


def select_kernel(place, blocks, out):
    for s in range(out.shape[0]):
        out[s] = blocks[place[1, s]]


def select(place, blocks, slots):
    shape = (slots,) + blocks.shape[1:]
    return pl.pallas_call(
        select_kernel,
        out_shape=jax.ShapeDtypeStruct(shape, blocks.dtype),
        in_specs=[
            pl.BlockSpec(memory_space=pltpu.SMEM),
            pl.BlockSpec(memory_space=pltpu.VMEM),
        ],
        out_specs=pl.BlockSpec(memory_space=pltpu.VMEM),
        compiler_params=LIMIT,
        cost_estimate=pl.CostEstimate(
            flops=0, bytes_accessed=2 * blocks.size, transcendentals=0
        ),
    )(place, blocks)


def contract_half(blocks, weights, half, total):
    each = 2 * GROUP
    depth = each * HALF
    for g in range(weights.shape[1] // depth):
        lhs = jnp.concatenate([blocks(g * each + s) for s in range(each)], axis=0)
        total += lax.dot_general(
            lhs,
            weights[half, pl.ds(g * depth, depth), :],
            (((0,), (0,)), ((), ())),
            preferred_element_type=jnp.float32,
        )
    return total


def first_kernel(place, blocks, weights, out):
    out[...] = contract_half(
        lambda s: blocks[place[0, s]], weights, 0, jnp.zeros(out.shape, jnp.float32)
    )


def second_kernel(blocks, weights, start, out):
    out[...] = contract_half(lambda s: blocks[s], weights, 1, start[...])


def first(place, blocks, weights):
    _, depth, cols = weights.shape
    rows = blocks.shape[-1]
    vmem = pl.BlockSpec(memory_space=pltpu.VMEM)
    return pl.pallas_call(
        first_kernel,
        out_shape=jax.ShapeDtypeStruct((rows, cols), jnp.float32),
        in_specs=[pl.BlockSpec(memory_space=pltpu.SMEM), vmem, vmem],
        out_specs=vmem,
        compiler_params=LIMIT,
        cost_estimate=pl.CostEstimate(
            flops=2 * depth * rows * cols, bytes_accessed=4 * 1024 * 1024, transcendentals=0
        ),
    )(place, blocks, weights)


def second(blocks, weights, start):
    _, depth, cols = weights.shape
    vmem = pl.BlockSpec(memory_space=pltpu.VMEM)
    return pl.pallas_call(
        second_kernel,
        out_shape=jax.ShapeDtypeStruct(start.shape, start.dtype),
        in_specs=[vmem, vmem, vmem],
        out_specs=vmem,
        compiler_params=LIMIT,
        cost_estimate=pl.CostEstimate(
            flops=2 * depth * start.size, bytes_accessed=2 * 1024 * 1024, transcendentals=0
        ),
    )(blocks, weights, start)


def body(amplitudes, block_tiles, block_rows, tile_mask, block_counts):
    slots = block_rows.shape[-1]
    cols_here = tile_mask.shape[-1] * BLOCK
    rows = amplitudes.shape[0]
    n_red = lax.axis_size("red")
    groups = server_groups()
    here = lax.axis_index("col").astype(jnp.int32)
    core = here & 1
    here = here.reshape(1)

    mine, send = front(amplitudes, block_rows[0], block_counts[0], here)
    given = lax.ppermute(send, "col", swap_pairs())
    chip = jnp.concatenate([mine, given[:-1]])
    sources = [chip] + [lax.ppermute(chip, "col", step_pairs(s)) for s in range(1, STEPS)]

    ask, place = requests(send[-1], given, here)
    asked = lax.all_to_all(
        ask, "col", split_axis=0, concat_axis=0, tiled=True, axis_index_groups=groups
    )

    alive = jnp.arange(slots) < block_counts[0, 0]
    keep = jnp.repeat(tile_mask[0, 0] * alive[:, None], BLOCK, axis=1).astype(jnp.bfloat16)
    weights = stack(core.reshape(1), block_tiles[0, 0], keep)
    asked, weights = lax.optimization_barrier((asked, weights))
    outgoing = pick(asked, sources)
    incoming = lax.all_to_all(
        outgoing.reshape(MEMBERS, -1, HALF, rows),
        "col",
        split_axis=0,
        concat_axis=0,
        tiled=True,
        axis_index_groups=groups,
    ).reshape(-1, HALF, rows)

    received = lax.ppermute(select(place, incoming, slots), "col", swap_pairs())
    partial_value = second(received, weights, first(place, incoming, weights))

    slices = partial_value.reshape(n_red, rows // n_red, cols_here)
    gathered = lax.all_to_all(slices, "red", split_axis=0, concat_axis=0, tiled=True)
    mine = jnp.sum(gathered, axis=0)
    copies = jnp.broadcast_to(mine[None], gathered.shape)
    whole = lax.all_to_all(copies, "red", split_axis=0, concat_axis=0, tiled=True)
    return whole.reshape(rows, cols_here)


def solution(mesh):
    placed = (
        P(None, ("red", "col")),
        P("red", "col", None, None),
        P("red", "col", None),
        P("red", "col", None, None),
        P("red", "col"),
    )
    return jax.shard_map(
        body, mesh=mesh, in_specs=placed, out_specs=P(None, "col"), check_vma=False
    )
```

```python
import jax
import jax.numpy as jnp
from jax import lax
from jax.experimental import pallas as pl
from jax.experimental.pallas import tpu as pltpu
from jax.sharding import PartitionSpec as P

BLOCK = 64
HALF = 32
CAP = 2
GROUP = 4
NY = 4
NZ = 8
NCORE = 2
STEPS = 4
ORDER = (0, 1, 3, 2)
MEMBERS = 8
LIMIT = pltpu.CompilerParams(vmem_limit_bytes=16 * 1024 * 1024)


def col_index(y, z, core):
    return (y % NY * NZ + z % NZ) * NCORE + core


def server_groups():
    along_z = [[col_index(y, z, 0) for z in range(NZ)] for y in range(NY)]
    along_y = [
        [col_index(y, 2 * pair + odd, 1) for y in range(NY) for odd in range(2)]
        for pair in range(NZ // 2)
    ]
    return along_z + along_y


def step_pairs(step):
    pairs = []
    for y in range(NY):
        for z in range(NZ):
            pairs.append((col_index(y + step, z, 0), col_index(y, z, 0)))
            pairs.append((col_index(y, z + 2 * step, 1), col_index(y, z, 1)))
    return pairs


def swap_pairs():
    return [(i, i ^ 1) for i in range(NY * NZ * NCORE)]


def front_kernel(here, count, amplitudes, rows, mine, send, note):
    core = here[0] & 1
    blocks_here = mine.shape[0]
    for pair in range(blocks_here // 2):
        width = 2 * BLOCK
        block = amplitudes[:, pl.ds(pair * width, width)].T
        for i in range(2):
            low = block[i * BLOCK : i * BLOCK + HALF]
            high = block[i * BLOCK + HALF : (i + 1) * BLOCK]
            mine[2 * pair + i] = jnp.where(core == 0, low, high)
            send[2 * pair + i] = jnp.where(core == 0, high, low)
    ids = rows[...]
    alive = lax.broadcasted_iota(jnp.int32, ids.shape, 1) < count[0]
    note[...] = jnp.zeros(note.shape, jnp.float32)
    note[0:1, : ids.shape[1]] = (ids >> 4).astype(jnp.float32)
    note[1:2, : ids.shape[1]] = jnp.where(alive, (ids & blocks_here - 1) + 1, 0).astype(jnp.float32)
    send[blocks_here] = note[...].astype(send.dtype)


def front(amplitudes, rows, count, here):
    lanes, columns = amplitudes.shape
    blocks_here = columns // BLOCK
    vmem = pl.BlockSpec(memory_space=pltpu.VMEM)
    smem = pl.BlockSpec(memory_space=pltpu.SMEM)
    return pl.pallas_call(
        front_kernel,
        out_shape=(
            jax.ShapeDtypeStruct((blocks_here, HALF, lanes), amplitudes.dtype),
            jax.ShapeDtypeStruct((blocks_here + 1, HALF, lanes), amplitudes.dtype),
        ),
        in_specs=[smem, smem, vmem, vmem],
        out_specs=(vmem, vmem),
        scratch_shapes=[pltpu.VMEM((HALF, lanes), jnp.float32)],
        compiler_params=LIMIT,
        cost_estimate=pl.CostEstimate(flops=0, bytes_accessed=4 * amplitudes.size, transcendentals=0),
    )(here, count, amplitudes, rows)


def requests_kernel(here, own, other, ask, place):
    core = here[0] & 1
    z = here[0] >> 1 & NZ - 1
    y = here[0] >> 4
    members, _, lanes = ask.shape
    per_member = NCORE * STEPS * NCORE * CAP
    square = (lanes, lanes)
    down = lax.broadcasted_iota(jnp.int32, square, 0)
    along = lax.broadcasted_iota(jnp.int32, square, 1)
    total = jnp.zeros((members, lanes), jnp.float32)
    for turn, note in enumerate((own[...], other[other.shape[0] - 1])):
        device = core if turn == 0 else 1 - core
        values = note.astype(jnp.float32)
        owner = values[0:1].astype(jnp.int32)
        index = values[1:2]
        wide = jnp.broadcast_to(values[0:1], square)
        live = jnp.broadcast_to(index, square)
        earlier = (wide.T == wide) & (down < along) & (live.T > 0.5)
        rank = jnp.sum(jnp.where(earlier, 1.0, 0.0), axis=0, keepdims=True).astype(jnp.int32)
        owner_z = owner >> 1 & NZ - 1
        owner_y = owner >> 4
        server = jnp.where(core == 0, owner_z, owner_y * 2 + (owner_z & 1))
        step = jnp.where(core == 0, owner_y - y, (owner_z >> 1) - (z >> 1)) & STEPS - 1
        within = ((device * STEPS + step) * NCORE + (owner & 1 ^ core)) * CAP + rank
        spot = server * per_member + within
        place[turn : turn + 1, :] = jnp.minimum(spot, members * per_member - 1)
        rows = lax.broadcasted_iota(jnp.int32, (members, lanes), 0)
        asked = jnp.where(rows == server, jnp.broadcast_to(index, (members, lanes)), 0.0)
        slot = jnp.where(down == within, 1.0, 0.0)
        total += lax.dot_general(
            asked.astype(jnp.bfloat16),
            slot.astype(jnp.bfloat16),
            (((1,), (1,)), ((), ())),
            preferred_element_type=jnp.float32,
        )
    found = total.astype(jnp.int32)
    for member in range(members):
        ask[member] = jnp.broadcast_to(found[member : member + 1], ask.shape[1:])


def requests(own, other, here):
    lanes = own.shape[-1]
    vmem = pl.BlockSpec(memory_space=pltpu.VMEM)
    return pl.pallas_call(
        requests_kernel,
        out_shape=(
            jax.ShapeDtypeStruct((MEMBERS, 8, lanes), jnp.int32),
            jax.ShapeDtypeStruct((8, lanes), jnp.int32),
        ),
        in_specs=[pl.BlockSpec(memory_space=pltpu.SMEM), vmem, vmem],
        out_specs=(vmem, vmem),
        compiler_params=LIMIT,
        cost_estimate=pl.CostEstimate(flops=0, bytes_accessed=65536, transcendentals=0),
    )(here, own, other)


def stack_kernel(mine, tiles, keep, out, buf, sem):
    slots, cols = keep.shape
    chunks, _, width = buf.shape
    each = slots // chunks

    def copy(i):
        return pltpu.make_async_copy(tiles.at[:, pl.ds(i * width, width)], buf.at[i], sem.at[i])

    for i in range(chunks):
        copy(i).start()
    for i in range(chunks):
        copy(i).wait()
        for part in range(2):
            half = mine[0] if part == 0 else 1 - mine[0]
            rows = pl.ds(pl.multiple_of(half * HALF, HALF), HALF)
            for j in range(each):
                s = i * each + j
                out[part, pl.ds(s * HALF, HALF), :] = (
                    buf[i, rows, pl.ds(j * cols, cols)] * keep[pl.ds(s, 1), :]
                )


def stack(mine, tiles, keep):
    slots, cols = keep.shape
    chunks = slots // GROUP
    return pl.pallas_call(
        stack_kernel,
        out_shape=jax.ShapeDtypeStruct((2, slots * HALF, cols), tiles.dtype),
        in_specs=[
            pl.BlockSpec(memory_space=pltpu.SMEM),
            pl.BlockSpec(memory_space=pl.ANY),
            pl.BlockSpec(memory_space=pltpu.VMEM),
        ],
        out_specs=pl.BlockSpec(memory_space=pltpu.VMEM),
        scratch_shapes=[
            pltpu.VMEM((chunks, BLOCK, GROUP * cols), tiles.dtype),
            pltpu.SemaphoreType.DMA((chunks,)),
        ],
        compiler_params=LIMIT,
        cost_estimate=pl.CostEstimate(
            flops=slots * BLOCK * cols, bytes_accessed=4 * slots * BLOCK * cols, transcendentals=0
        ),
    )(mine, tiles, keep)


def pick_kernel(asked, *refs):
    *sources, out = refs
    members = asked.shape[0]
    per_member = out.shape[0] // members
    blocks_here = sources[0].shape[0] // NCORE
    for member in range(members):
        for slot in range(per_member):
            step = slot % (STEPS * NCORE * CAP) // (NCORE * CAP)
            core = slot // CAP % NCORE
            block = jnp.maximum(asked[member, 0, slot] - 1, 0)
            out[member * per_member + slot] = sources[ORDER.index(step)][core * blocks_here + block]


def pick(asked, sources):
    members = asked.shape[0]
    slots = members * NCORE * STEPS * NCORE * CAP
    shape = (slots,) + sources[0].shape[1:]
    return pl.pallas_call(
        pick_kernel,
        out_shape=jax.ShapeDtypeStruct(shape, sources[0].dtype),
        in_specs=[pl.BlockSpec(memory_space=pltpu.SMEM)]
        + [pl.BlockSpec(memory_space=pltpu.VMEM)] * len(sources),
        out_specs=pl.BlockSpec(memory_space=pltpu.VMEM),
        compiler_params=LIMIT,
        cost_estimate=pl.CostEstimate(
            flops=0, bytes_accessed=4 * slots * HALF * shape[-1], transcendentals=0
        ),
    )(asked, *sources)


def select_kernel(place, blocks, out):
    for s in range(out.shape[0]):
        out[s] = blocks[place[1, s]]


def select(place, blocks, slots):
    shape = (slots,) + blocks.shape[1:]
    return pl.pallas_call(
        select_kernel,
        out_shape=jax.ShapeDtypeStruct(shape, blocks.dtype),
        in_specs=[
            pl.BlockSpec(memory_space=pltpu.SMEM),
            pl.BlockSpec(memory_space=pltpu.VMEM),
        ],
        out_specs=pl.BlockSpec(memory_space=pltpu.VMEM),
        compiler_params=LIMIT,
        cost_estimate=pl.CostEstimate(
            flops=0, bytes_accessed=2 * blocks.size, transcendentals=0
        ),
    )(place, blocks)


def contract_half(blocks, weights, half, total):
    each = 2 * GROUP
    depth = each * HALF
    for g in range(weights.shape[1] // depth):
        lhs = jnp.concatenate([blocks(g * each + s) for s in range(each)], axis=0)
        total += lax.dot_general(
            lhs,
            weights[half, pl.ds(g * depth, depth), :],
            (((0,), (0,)), ((), ())),
            preferred_element_type=jnp.float32,
        )
    return total


def first_kernel(place, blocks, weights, out):
    out[...] = contract_half(
        lambda s: blocks[place[0, s]], weights, 0, jnp.zeros(out.shape, jnp.float32)
    )


def second_kernel(blocks, weights, start, out):
    out[...] = contract_half(lambda s: blocks[s], weights, 1, start[...])


def first(place, blocks, weights):
    _, depth, cols = weights.shape
    rows = blocks.shape[-1]
    vmem = pl.BlockSpec(memory_space=pltpu.VMEM)
    return pl.pallas_call(
        first_kernel,
        out_shape=jax.ShapeDtypeStruct((rows, cols), jnp.float32),
        in_specs=[pl.BlockSpec(memory_space=pltpu.SMEM), vmem, vmem],
        out_specs=vmem,
        compiler_params=LIMIT,
        cost_estimate=pl.CostEstimate(
            flops=2 * depth * rows * cols, bytes_accessed=4 * 1024 * 1024, transcendentals=0
        ),
    )(place, blocks, weights)


def second(blocks, weights, start):
    _, depth, cols = weights.shape
    vmem = pl.BlockSpec(memory_space=pltpu.VMEM)
    return pl.pallas_call(
        second_kernel,
        out_shape=jax.ShapeDtypeStruct(start.shape, start.dtype),
        in_specs=[vmem, vmem, vmem],
        out_specs=vmem,
        compiler_params=LIMIT,
        cost_estimate=pl.CostEstimate(
            flops=2 * depth * start.size, bytes_accessed=2 * 1024 * 1024, transcendentals=0
        ),
    )(blocks, weights, start)


def body(amplitudes, block_tiles, block_rows, tile_mask, block_counts):
    slots = block_rows.shape[-1]
    cols_here = tile_mask.shape[-1] * BLOCK
    rows = amplitudes.shape[0]
    n_red = lax.axis_size("red")
    groups = server_groups()
    here = lax.axis_index("col").astype(jnp.int32)
    core = here & 1
    here = here.reshape(1)

    mine, send = front(amplitudes, block_rows[0], block_counts[0], here)
    given = lax.ppermute(send, "col", swap_pairs())
    chip = jnp.concatenate([mine, given[:-1]])
    sources = [chip] + [lax.ppermute(chip, "col", step_pairs(s)) for s in ORDER[1:]]

    ask, place = requests(send[-1], given, here)
    asked = lax.all_to_all(
        ask, "col", split_axis=0, concat_axis=0, tiled=True, axis_index_groups=groups
    )

    alive = jnp.arange(slots) < block_counts[0, 0]
    keep = jnp.repeat(tile_mask[0, 0] * alive[:, None], BLOCK, axis=1).astype(jnp.bfloat16)
    weights = stack(core.reshape(1), block_tiles[0, 0], keep)
    asked, weights = lax.optimization_barrier((asked, weights))
    outgoing = pick(asked, sources)
    incoming = lax.all_to_all(
        outgoing.reshape(MEMBERS, -1, HALF, rows),
        "col",
        split_axis=0,
        concat_axis=0,
        tiled=True,
        axis_index_groups=groups,
    ).reshape(-1, HALF, rows)

    received = lax.ppermute(select(place, incoming, slots), "col", swap_pairs())
    partial_value = second(received, weights, first(place, incoming, weights))

    slices = partial_value.reshape(n_red, rows // n_red, cols_here)
    gathered = lax.all_to_all(slices, "red", split_axis=0, concat_axis=0, tiled=True)
    mine = jnp.sum(gathered, axis=0)
    copies = jnp.broadcast_to(mine[None], gathered.shape)
    whole = lax.all_to_all(copies, "red", split_axis=0, concat_axis=0, tiled=True)
    return whole.reshape(rows, cols_here)


def solution(mesh):
    placed = (
        P(None, ("red", "col")),
        P("red", "col", None, None),
        P("red", "col", None),
        P("red", "col", None, None),
        P("red", "col"),
    )
    return jax.shard_map(
        body, mesh=mesh, in_specs=placed, out_specs=P(None, "col"), check_vma=False
    )
```

```python
import jax
import jax.numpy as jnp
from jax import lax
from jax.experimental import pallas as pl
from jax.experimental.pallas import tpu as pltpu
from jax.sharding import PartitionSpec as P

BLOCK = 64
HALF = 32
CAP = 2
GROUP = 4
NY = 4
NZ = 8
NCORE = 2
STEPS = 4
ORDER = (0, 1, 3, 2)
MEMBERS = 8
LIMIT = pltpu.CompilerParams(vmem_limit_bytes=16 * 1024 * 1024)


def col_index(y, z, core):
    return (y % NY * NZ + z % NZ) * NCORE + core


def server_groups():
    along_z = [[col_index(y, z, 0) for z in range(NZ)] for y in range(NY)]
    along_y = [
        [col_index(y, 2 * pair + odd, 1) for y in range(NY) for odd in range(2)]
        for pair in range(NZ // 2)
    ]
    return along_z + along_y


def step_pairs(step):
    pairs = []
    for y in range(NY):
        for z in range(NZ):
            pairs.append((col_index(y + step, z, 0), col_index(y, z, 0)))
            pairs.append((col_index(y, z + 2 * step, 1), col_index(y, z, 1)))
    return pairs


def swap_pairs():
    return [(i, i ^ 1) for i in range(NY * NZ * NCORE)]


def front_kernel(here, count, amplitudes, rows, mine, send, note):
    core = here[0] & 1
    blocks_here = mine.shape[0]
    for pair in range(blocks_here // 2):
        width = 2 * BLOCK
        block = amplitudes[:, pl.ds(pair * width, width)].T
        for i in range(2):
            low = block[i * BLOCK : i * BLOCK + HALF]
            high = block[i * BLOCK + HALF : (i + 1) * BLOCK]
            mine[2 * pair + i] = jnp.where(core == 0, low, high)
            send[2 * pair + i] = jnp.where(core == 0, high, low)
    ids = rows[...]
    alive = lax.broadcasted_iota(jnp.int32, ids.shape, 1) < count[0]
    note[...] = jnp.zeros(note.shape, jnp.float32)
    note[0:1, : ids.shape[1]] = (ids >> 4).astype(jnp.float32)
    note[1:2, : ids.shape[1]] = jnp.where(alive, (ids & blocks_here - 1) + 1, 0).astype(jnp.float32)
    send[blocks_here] = note[...].astype(send.dtype)


def front(amplitudes, rows, count, here):
    lanes, columns = amplitudes.shape
    blocks_here = columns // BLOCK
    vmem = pl.BlockSpec(memory_space=pltpu.VMEM)
    smem = pl.BlockSpec(memory_space=pltpu.SMEM)
    return pl.pallas_call(
        front_kernel,
        out_shape=(
            jax.ShapeDtypeStruct((blocks_here, HALF, lanes), amplitudes.dtype),
            jax.ShapeDtypeStruct((blocks_here + 1, HALF, lanes), amplitudes.dtype),
        ),
        in_specs=[smem, smem, vmem, vmem],
        out_specs=(vmem, vmem),
        scratch_shapes=[pltpu.VMEM((HALF, lanes), jnp.float32)],
        compiler_params=LIMIT,
        cost_estimate=pl.CostEstimate(flops=0, bytes_accessed=4 * amplitudes.size, transcendentals=0),
    )(here, count, amplitudes, rows)


def requests_kernel(here, own, other, ask, place):
    core = here[0] & 1
    z = here[0] >> 1 & NZ - 1
    y = here[0] >> 4
    members, _, lanes = ask.shape
    per_member = NCORE * STEPS * NCORE * CAP
    square = (lanes, lanes)
    down = lax.broadcasted_iota(jnp.int32, square, 0)
    along = lax.broadcasted_iota(jnp.int32, square, 1)
    total = jnp.zeros((members, lanes), jnp.float32)
    for turn, note in enumerate((own[...], other[other.shape[0] - 1])):
        device = core if turn == 0 else 1 - core
        values = note.astype(jnp.float32)
        owner = values[0:1].astype(jnp.int32)
        index = values[1:2]
        wide = jnp.broadcast_to(values[0:1], square)
        live = jnp.broadcast_to(index, square)
        earlier = (wide.T == wide) & (down < along) & (live.T > 0.5)
        rank = jnp.sum(jnp.where(earlier, 1.0, 0.0), axis=0, keepdims=True).astype(jnp.int32)
        owner_z = owner >> 1 & NZ - 1
        owner_y = owner >> 4
        server = jnp.where(core == 0, owner_z, owner_y * 2 + (owner_z & 1))
        step = jnp.where(core == 0, owner_y - y, (owner_z >> 1) - (z >> 1)) & STEPS - 1
        within = ((device * STEPS + step) * NCORE + (owner & 1 ^ core)) * CAP + rank
        spot = server * per_member + within
        place[turn : turn + 1, :] = jnp.minimum(spot, members * per_member - 1)
        rows = lax.broadcasted_iota(jnp.int32, (members, lanes), 0)
        asked = jnp.where(rows == server, jnp.broadcast_to(index, (members, lanes)), 0.0)
        slot = jnp.where(down == within, 1.0, 0.0)
        total += lax.dot_general(
            asked.astype(jnp.bfloat16),
            slot.astype(jnp.bfloat16),
            (((1,), (1,)), ((), ())),
            preferred_element_type=jnp.float32,
        )
    found = total.astype(jnp.int32)
    for member in range(members):
        ask[member] = jnp.broadcast_to(found[member : member + 1], ask.shape[1:])


def requests(own, other, here):
    lanes = own.shape[-1]
    vmem = pl.BlockSpec(memory_space=pltpu.VMEM)
    return pl.pallas_call(
        requests_kernel,
        out_shape=(
            jax.ShapeDtypeStruct((MEMBERS, 1, lanes), jnp.int32),
            jax.ShapeDtypeStruct((8, lanes), jnp.int32),
        ),
        in_specs=[pl.BlockSpec(memory_space=pltpu.SMEM), vmem, vmem],
        out_specs=(vmem, vmem),
        compiler_params=LIMIT,
        cost_estimate=pl.CostEstimate(flops=0, bytes_accessed=65536, transcendentals=0),
    )(here, own, other)


def stack_kernel(mine, tiles, keep, out, buf, sem):
    slots, cols = keep.shape
    chunks, _, width = buf.shape
    each = slots // chunks

    def copy(i):
        return pltpu.make_async_copy(tiles.at[:, pl.ds(i * width, width)], buf.at[i], sem.at[i])

    for i in range(chunks):
        copy(i).start()
    for i in range(chunks):
        copy(i).wait()
        for part in range(2):
            half = mine[0] if part == 0 else 1 - mine[0]
            rows = pl.ds(pl.multiple_of(half * HALF, HALF), HALF)
            for j in range(each):
                s = i * each + j
                out[part, pl.ds(s * HALF, HALF), :] = (
                    buf[i, rows, pl.ds(j * cols, cols)] * keep[pl.ds(s, 1), :]
                )


def stack(mine, tiles, keep):
    slots, cols = keep.shape
    chunks = slots // GROUP
    return pl.pallas_call(
        stack_kernel,
        out_shape=jax.ShapeDtypeStruct((2, slots * HALF, cols), tiles.dtype),
        in_specs=[
            pl.BlockSpec(memory_space=pltpu.SMEM),
            pl.BlockSpec(memory_space=pl.ANY),
            pl.BlockSpec(memory_space=pltpu.VMEM),
        ],
        out_specs=pl.BlockSpec(memory_space=pltpu.VMEM),
        scratch_shapes=[
            pltpu.VMEM((chunks, BLOCK, GROUP * cols), tiles.dtype),
            pltpu.SemaphoreType.DMA((chunks,)),
        ],
        compiler_params=LIMIT,
        cost_estimate=pl.CostEstimate(
            flops=slots * BLOCK * cols, bytes_accessed=4 * slots * BLOCK * cols, transcendentals=0
        ),
    )(mine, tiles, keep)


def pick_kernel(asked, *refs):
    *sources, out = refs
    members = asked.shape[0]
    per_member = out.shape[0] // members
    blocks_here = sources[0].shape[0] // NCORE
    for member in range(members):
        for slot in range(per_member):
            step = slot % (STEPS * NCORE * CAP) // (NCORE * CAP)
            core = slot // CAP % NCORE
            block = jnp.maximum(asked[member, 0, slot] - 1, 0)
            out[member * per_member + slot] = sources[ORDER.index(step)][core * blocks_here + block]


def pick(asked, sources):
    members = asked.shape[0]
    slots = members * NCORE * STEPS * NCORE * CAP
    shape = (slots,) + sources[0].shape[1:]
    return pl.pallas_call(
        pick_kernel,
        out_shape=jax.ShapeDtypeStruct(shape, sources[0].dtype),
        in_specs=[pl.BlockSpec(memory_space=pltpu.SMEM)]
        + [pl.BlockSpec(memory_space=pltpu.VMEM)] * len(sources),
        out_specs=pl.BlockSpec(memory_space=pltpu.VMEM),
        compiler_params=LIMIT,
        cost_estimate=pl.CostEstimate(
            flops=0, bytes_accessed=4 * slots * HALF * shape[-1], transcendentals=0
        ),
    )(asked, *sources)


def select_kernel(place, blocks, out):
    for s in range(out.shape[0]):
        out[s] = blocks[place[1, s]]


def select(place, blocks, slots):
    shape = (slots,) + blocks.shape[1:]
    return pl.pallas_call(
        select_kernel,
        out_shape=jax.ShapeDtypeStruct(shape, blocks.dtype),
        in_specs=[
            pl.BlockSpec(memory_space=pltpu.SMEM),
            pl.BlockSpec(memory_space=pltpu.VMEM),
        ],
        out_specs=pl.BlockSpec(memory_space=pltpu.VMEM),
        compiler_params=LIMIT,
        cost_estimate=pl.CostEstimate(
            flops=0, bytes_accessed=2 * blocks.size, transcendentals=0
        ),
    )(place, blocks)


def contract_half(blocks, weights, half, total):
    each = 2 * GROUP
    depth = each * HALF
    for g in range(weights.shape[1] // depth):
        lhs = jnp.concatenate([blocks(g * each + s) for s in range(each)], axis=0)
        total += lax.dot_general(
            lhs,
            weights[half, pl.ds(g * depth, depth), :],
            (((0,), (0,)), ((), ())),
            preferred_element_type=jnp.float32,
        )
    return total


def first_kernel(place, blocks, weights, out):
    out[...] = contract_half(
        lambda s: blocks[place[0, s]], weights, 0, jnp.zeros(out.shape, jnp.float32)
    )


def second_kernel(blocks, weights, start, out):
    out[...] = contract_half(lambda s: blocks[s], weights, 1, start[...])


def first(place, blocks, weights):
    _, depth, cols = weights.shape
    rows = blocks.shape[-1]
    vmem = pl.BlockSpec(memory_space=pltpu.VMEM)
    return pl.pallas_call(
        first_kernel,
        out_shape=jax.ShapeDtypeStruct((rows, cols), jnp.float32),
        in_specs=[pl.BlockSpec(memory_space=pltpu.SMEM), vmem, vmem],
        out_specs=vmem,
        compiler_params=LIMIT,
        cost_estimate=pl.CostEstimate(
            flops=2 * depth * rows * cols, bytes_accessed=4 * 1024 * 1024, transcendentals=0
        ),
    )(place, blocks, weights)


def second(blocks, weights, start):
    _, depth, cols = weights.shape
    vmem = pl.BlockSpec(memory_space=pltpu.VMEM)
    return pl.pallas_call(
        second_kernel,
        out_shape=jax.ShapeDtypeStruct(start.shape, start.dtype),
        in_specs=[vmem, vmem, vmem],
        out_specs=vmem,
        compiler_params=LIMIT,
        cost_estimate=pl.CostEstimate(
            flops=2 * depth * start.size, bytes_accessed=2 * 1024 * 1024, transcendentals=0
        ),
    )(blocks, weights, start)


def body(amplitudes, block_tiles, block_rows, tile_mask, block_counts):
    slots = block_rows.shape[-1]
    cols_here = tile_mask.shape[-1] * BLOCK
    rows = amplitudes.shape[0]
    n_red = lax.axis_size("red")
    groups = server_groups()
    here = lax.axis_index("col").astype(jnp.int32)
    core = here & 1
    here = here.reshape(1)

    mine, send = front(amplitudes, block_rows[0], block_counts[0], here)
    given = lax.ppermute(send, "col", swap_pairs())
    chip = jnp.concatenate([mine, given[:-1]])
    sources = [chip] + [lax.ppermute(chip, "col", step_pairs(s)) for s in ORDER[1:]]

    ask, place = requests(send[-1], given, here)
    asked = lax.all_to_all(
        ask, "col", split_axis=0, concat_axis=0, tiled=True, axis_index_groups=groups
    )

    alive = jnp.arange(slots) < block_counts[0, 0]
    keep = jnp.repeat(tile_mask[0, 0] * alive[:, None], BLOCK, axis=1).astype(jnp.bfloat16)
    weights = stack(core.reshape(1), block_tiles[0, 0], keep)
    asked, weights = lax.optimization_barrier((asked, weights))
    outgoing = pick(asked, sources)
    incoming = lax.all_to_all(
        outgoing.reshape(MEMBERS, -1, HALF, rows),
        "col",
        split_axis=0,
        concat_axis=0,
        tiled=True,
        axis_index_groups=groups,
    ).reshape(-1, HALF, rows)

    received = lax.ppermute(select(place, incoming, slots), "col", swap_pairs())
    partial_value = second(received, weights, first(place, incoming, weights))

    slices = partial_value.reshape(n_red, rows // n_red, cols_here)
    gathered = lax.all_to_all(slices, "red", split_axis=0, concat_axis=0, tiled=True)
    mine = jnp.sum(gathered, axis=0)
    copies = jnp.broadcast_to(mine[None], gathered.shape)
    whole = lax.all_to_all(copies, "red", split_axis=0, concat_axis=0, tiled=True)
    return whole.reshape(rows, cols_here)


def solution(mesh):
    placed = (
        P(None, ("red", "col")),
        P("red", "col", None, None),
        P("red", "col", None),
        P("red", "col", None, None),
        P("red", "col"),
    )
    return jax.shard_map(
        body, mesh=mesh, in_specs=placed, out_specs=P(None, "col"), check_vma=False
    )
```

```python
import jax
import jax.numpy as jnp
from jax import lax
from jax.experimental import pallas as pl
from jax.experimental.pallas import tpu as pltpu
from jax.sharding import PartitionSpec as P

BLOCK = 64
HALF = 32
CAP = 2
GROUP = 4
NY = 4
NZ = 8
NCORE = 2
STEPS = 4
ORDER = (0, 1, 3, 2)
MEMBERS = 8
LIMIT = pltpu.CompilerParams(vmem_limit_bytes=16 * 1024 * 1024)


def col_index(y, z, core):
    return (y % NY * NZ + z % NZ) * NCORE + core


def server_groups():
    along_z = [[col_index(y, z, 0) for z in range(NZ)] for y in range(NY)]
    along_y = [
        [col_index(y, 2 * pair + odd, 1) for y in range(NY) for odd in range(2)]
        for pair in range(NZ // 2)
    ]
    return along_z + along_y


def step_pairs(step):
    pairs = []
    for y in range(NY):
        for z in range(NZ):
            pairs.append((col_index(y + step, z, 0), col_index(y, z, 0)))
            pairs.append((col_index(y, z + 2 * step, 1), col_index(y, z, 1)))
    return pairs


def swap_pairs():
    return [(i, i ^ 1) for i in range(NY * NZ * NCORE)]


def front_kernel(here, count, amplitudes, rows, mine, send, note):
    core = here[0] & 1
    blocks_here = mine.shape[0]
    for pair in range(blocks_here // 2):
        width = 2 * BLOCK
        block = amplitudes[:, pl.ds(pair * width, width)].T
        for i in range(2):
            low = block[i * BLOCK : i * BLOCK + HALF]
            high = block[i * BLOCK + HALF : (i + 1) * BLOCK]
            mine[2 * pair + i] = jnp.where(core == 0, low, high)
            send[2 * pair + i] = jnp.where(core == 0, high, low)
    ids = rows[...]
    alive = lax.broadcasted_iota(jnp.int32, ids.shape, 1) < count[0]
    note[...] = jnp.zeros(note.shape, jnp.float32)
    note[0:1, : ids.shape[1]] = (ids >> 4).astype(jnp.float32)
    note[1:2, : ids.shape[1]] = jnp.where(alive, (ids & blocks_here - 1) + 1, 0).astype(jnp.float32)
    send[blocks_here] = note[...].astype(send.dtype)


def front(amplitudes, rows, count, here):
    lanes, columns = amplitudes.shape
    blocks_here = columns // BLOCK
    vmem = pl.BlockSpec(memory_space=pltpu.VMEM)
    smem = pl.BlockSpec(memory_space=pltpu.SMEM)
    return pl.pallas_call(
        front_kernel,
        out_shape=(
            jax.ShapeDtypeStruct((blocks_here, HALF, lanes), amplitudes.dtype),
            jax.ShapeDtypeStruct((blocks_here + 1, HALF, lanes), amplitudes.dtype),
        ),
        in_specs=[smem, smem, vmem, vmem],
        out_specs=(vmem, vmem),
        scratch_shapes=[pltpu.VMEM((HALF, lanes), jnp.float32)],
        compiler_params=LIMIT,
        cost_estimate=pl.CostEstimate(flops=0, bytes_accessed=4 * amplitudes.size, transcendentals=0),
    )(here, count, amplitudes, rows)


def requests_kernel(here, own, other, ask, place):
    core = here[0] & 1
    z = here[0] >> 1 & NZ - 1
    y = here[0] >> 4
    members, _, lanes = ask.shape
    per_member = NCORE * STEPS * NCORE * CAP
    square = (lanes, lanes)
    down = lax.broadcasted_iota(jnp.int32, square, 0)
    along = lax.broadcasted_iota(jnp.int32, square, 1)
    total = jnp.zeros((members, lanes), jnp.float32)
    for turn, note in enumerate((own[...], other[other.shape[0] - 1])):
        device = core if turn == 0 else 1 - core
        values = note.astype(jnp.float32)
        owner = values[0:1].astype(jnp.int32)
        index = values[1:2]
        wide = jnp.broadcast_to(values[0:1], square)
        live = jnp.broadcast_to(index, square)
        earlier = (wide.T == wide) & (down < along) & (live.T > 0.5)
        rank = jnp.sum(jnp.where(earlier, 1.0, 0.0), axis=0, keepdims=True).astype(jnp.int32)
        owner_z = owner >> 1 & NZ - 1
        owner_y = owner >> 4
        server = jnp.where(core == 0, owner_z, owner_y * 2 + (owner_z & 1))
        step = jnp.where(core == 0, owner_y - y, (owner_z >> 1) - (z >> 1)) & STEPS - 1
        within = ((device * STEPS + step) * NCORE + (owner & 1 ^ core)) * CAP + rank
        spot = server * per_member + within
        place[turn : turn + 1, :] = jnp.minimum(spot, members * per_member - 1)
        rows = lax.broadcasted_iota(jnp.int32, (members, lanes), 0)
        asked = jnp.where(rows == server, jnp.broadcast_to(index, (members, lanes)), 0.0)
        slot = jnp.where(down == within, 1.0, 0.0)
        total += lax.dot_general(
            asked.astype(jnp.bfloat16),
            slot.astype(jnp.bfloat16),
            (((1,), (1,)), ((), ())),
            preferred_element_type=jnp.float32,
        )
    found = total.astype(jnp.int32)
    for member in range(members):
        ask[member] = jnp.broadcast_to(found[member : member + 1], ask.shape[1:])


def requests(own, other, here):
    lanes = own.shape[-1]
    vmem = pl.BlockSpec(memory_space=pltpu.VMEM)
    return pl.pallas_call(
        requests_kernel,
        out_shape=(
            jax.ShapeDtypeStruct((MEMBERS, 1, lanes), jnp.int32),
            jax.ShapeDtypeStruct((8, lanes), jnp.int32),
        ),
        in_specs=[pl.BlockSpec(memory_space=pltpu.SMEM), vmem, vmem],
        out_specs=(vmem, vmem),
        compiler_params=LIMIT,
        cost_estimate=pl.CostEstimate(flops=0, bytes_accessed=65536, transcendentals=0),
    )(here, own, other)


def stack_kernel(mine, tiles, keep, out, buf, sem):
    slots, cols = keep.shape
    chunks, _, width = buf.shape
    each = slots // chunks

    def copy(i):
        return pltpu.make_async_copy(tiles.at[:, pl.ds(i * width, width)], buf.at[i], sem.at[i])

    for i in range(chunks):
        copy(i).start()
    for i in range(chunks):
        copy(i).wait()
        for part in range(2):
            half = mine[0] if part == 0 else 1 - mine[0]
            rows = pl.ds(pl.multiple_of(half * HALF, HALF), HALF)
            for j in range(each):
                s = i * each + j
                out[part, pl.ds(s * HALF, HALF), :] = (
                    buf[i, rows, pl.ds(j * cols, cols)] * keep[pl.ds(s, 1), :]
                )


def stack(mine, tiles, keep):
    slots, cols = keep.shape
    chunks = slots // GROUP
    return pl.pallas_call(
        stack_kernel,
        out_shape=jax.ShapeDtypeStruct((2, slots * HALF, cols), tiles.dtype),
        in_specs=[
            pl.BlockSpec(memory_space=pltpu.SMEM),
            pl.BlockSpec(memory_space=pl.ANY),
            pl.BlockSpec(memory_space=pltpu.VMEM),
        ],
        out_specs=pl.BlockSpec(memory_space=pltpu.VMEM),
        scratch_shapes=[
            pltpu.VMEM((chunks, BLOCK, GROUP * cols), tiles.dtype),
            pltpu.SemaphoreType.DMA((chunks,)),
        ],
        compiler_params=LIMIT,
        cost_estimate=pl.CostEstimate(
            flops=slots * BLOCK * cols, bytes_accessed=4 * slots * BLOCK * cols, transcendentals=0
        ),
    )(mine, tiles, keep)


def pick_kernel(asked, *refs):
    *sources, out = refs
    members = asked.shape[0]
    per_member = out.shape[0] // members
    blocks_here = sources[0].shape[0] // NCORE
    for member in range(members):
        for slot in range(per_member):
            step = slot % (STEPS * NCORE * CAP) // (NCORE * CAP)
            core = slot // CAP % NCORE
            block = jnp.maximum(asked[member, 0, slot] - 1, 0)
            out[member * per_member + slot] = sources[ORDER.index(step)][core * blocks_here + block]


def pick(asked, sources):
    members = asked.shape[0]
    slots = members * NCORE * STEPS * NCORE * CAP
    shape = (slots,) + sources[0].shape[1:]
    return pl.pallas_call(
        pick_kernel,
        out_shape=jax.ShapeDtypeStruct(shape, sources[0].dtype),
        in_specs=[pl.BlockSpec(memory_space=pltpu.SMEM)]
        + [pl.BlockSpec(memory_space=pltpu.VMEM)] * len(sources),
        out_specs=pl.BlockSpec(memory_space=pltpu.VMEM),
        compiler_params=LIMIT,
        cost_estimate=pl.CostEstimate(
            flops=0, bytes_accessed=4 * slots * HALF * shape[-1], transcendentals=0
        ),
    )(asked, *sources)


def select_kernel(place, blocks, out):
    for s in range(out.shape[0]):
        out[s] = blocks[place[1, s]]


def select(place, blocks, slots):
    shape = (slots,) + blocks.shape[1:]
    return pl.pallas_call(
        select_kernel,
        out_shape=jax.ShapeDtypeStruct(shape, blocks.dtype),
        in_specs=[
            pl.BlockSpec(memory_space=pltpu.SMEM),
            pl.BlockSpec(memory_space=pltpu.VMEM),
        ],
        out_specs=pl.BlockSpec(memory_space=pltpu.VMEM),
        compiler_params=LIMIT,
        cost_estimate=pl.CostEstimate(
            flops=0, bytes_accessed=2 * blocks.size, transcendentals=0
        ),
    )(place, blocks)


def contract_half(blocks, weights, half, total):
    each = 2 * GROUP
    depth = each * HALF
    for g in range(weights.shape[1] // depth):
        lhs = jnp.concatenate([blocks(g * each + s) for s in range(each)], axis=0)
        total += lax.dot_general(
            lhs,
            weights[half, pl.ds(g * depth, depth), :],
            (((0,), (0,)), ((), ())),
            preferred_element_type=jnp.float32,
        )
    return total


def first_kernel(place, blocks, weights, out):
    out[...] = contract_half(
        lambda s: blocks[place[0, s]], weights, 0, jnp.zeros(out.shape, jnp.float32)
    )


def second_kernel(blocks, weights, start, out):
    out[...] = contract_half(lambda s: blocks[s], weights, 1, start[...])


def first(place, blocks, weights):
    _, depth, cols = weights.shape
    rows = blocks.shape[-1]
    vmem = pl.BlockSpec(memory_space=pltpu.VMEM)
    return pl.pallas_call(
        first_kernel,
        out_shape=jax.ShapeDtypeStruct((rows, cols), jnp.float32),
        in_specs=[pl.BlockSpec(memory_space=pltpu.SMEM), vmem, vmem],
        out_specs=vmem,
        compiler_params=LIMIT,
        cost_estimate=pl.CostEstimate(
            flops=2 * depth * rows * cols, bytes_accessed=4 * 1024 * 1024, transcendentals=0
        ),
    )(place, blocks, weights)


def second(blocks, weights, start):
    _, depth, cols = weights.shape
    vmem = pl.BlockSpec(memory_space=pltpu.VMEM)
    return pl.pallas_call(
        second_kernel,
        out_shape=jax.ShapeDtypeStruct(start.shape, start.dtype),
        in_specs=[vmem, vmem, vmem],
        out_specs=vmem,
        compiler_params=LIMIT,
        cost_estimate=pl.CostEstimate(
            flops=2 * depth * start.size, bytes_accessed=2 * 1024 * 1024, transcendentals=0
        ),
    )(blocks, weights, start)


def body(amplitudes, block_tiles, block_rows, tile_mask, block_counts):
    slots = block_rows.shape[-1]
    cols_here = tile_mask.shape[-1] * BLOCK
    rows = amplitudes.shape[0]
    n_red = lax.axis_size("red")
    groups = server_groups()
    here = lax.axis_index("col").astype(jnp.int32)
    core = here & 1
    here = here.reshape(1)

    mine, send = front(amplitudes, block_rows[0], block_counts[0], here)
    given = lax.ppermute(send, "col", swap_pairs())
    alive = jnp.arange(slots) < block_counts[0, 0]
    keep = jnp.repeat(tile_mask[0, 0] * alive[:, None], BLOCK, axis=1).astype(jnp.bfloat16)
    given, keep = lax.optimization_barrier((given, keep))
    chip = jnp.concatenate([mine, given[:-1]])
    sources = [chip] + [lax.ppermute(chip, "col", step_pairs(s)) for s in ORDER[1:]]

    ask, place = requests(send[-1], given, here)
    asked = lax.all_to_all(
        ask, "col", split_axis=0, concat_axis=0, tiled=True, axis_index_groups=groups
    )

    weights = stack(core.reshape(1), block_tiles[0, 0], keep)
    asked, weights = lax.optimization_barrier((asked, weights))
    outgoing = pick(asked, sources)
    incoming = lax.all_to_all(
        outgoing.reshape(MEMBERS, -1, HALF, rows),
        "col",
        split_axis=0,
        concat_axis=0,
        tiled=True,
        axis_index_groups=groups,
    ).reshape(-1, HALF, rows)

    received = lax.ppermute(select(place, incoming, slots), "col", swap_pairs())
    partial_value = second(received, weights, first(place, incoming, weights))

    slices = partial_value.reshape(n_red, rows // n_red, cols_here)
    gathered = lax.all_to_all(slices, "red", split_axis=0, concat_axis=0, tiled=True)
    mine = jnp.sum(gathered, axis=0)
    copies = jnp.broadcast_to(mine[None], gathered.shape)
    whole = lax.all_to_all(copies, "red", split_axis=0, concat_axis=0, tiled=True)
    return whole.reshape(rows, cols_here)


def solution(mesh):
    placed = (
        P(None, ("red", "col")),
        P("red", "col", None, None),
        P("red", "col", None),
        P("red", "col", None, None),
        P("red", "col"),
    )
    return jax.shard_map(
        body, mesh=mesh, in_specs=placed, out_specs=P(None, "col"), check_vma=False
    )
```

```python
import jax
import jax.numpy as jnp
from jax import lax
from jax.experimental import pallas as pl
from jax.experimental.pallas import tpu as pltpu
from jax.sharding import PartitionSpec as P

BLOCK = 64
HALF = 32
CAP = 2
GROUP = 4
NY = 4
NZ = 8
NCORE = 2
STEPS = 4
ORDER = (0, 3, 1, 2)
MEMBERS = 8
LIMIT = pltpu.CompilerParams(vmem_limit_bytes=16 * 1024 * 1024)


def col_index(y, z, core):
    return (y % NY * NZ + z % NZ) * NCORE + core


def server_groups():
    along_z = [[col_index(y, z, 0) for z in range(NZ)] for y in range(NY)]
    along_y = [
        [col_index(y, 2 * pair + odd, 1) for y in range(NY) for odd in range(2)]
        for pair in range(NZ // 2)
    ]
    return along_z + along_y


def step_pairs(step):
    pairs = []
    for y in range(NY):
        for z in range(NZ):
            pairs.append((col_index(y + step, z, 0), col_index(y, z, 0)))
            pairs.append((col_index(y, z + 2 * step, 1), col_index(y, z, 1)))
    return pairs


def swap_pairs():
    return [(i, i ^ 1) for i in range(NY * NZ * NCORE)]


def front_kernel(here, count, amplitudes, rows, mine, send, note):
    core = here[0] & 1
    blocks_here = mine.shape[0]
    for pair in range(blocks_here // 2):
        width = 2 * BLOCK
        block = amplitudes[:, pl.ds(pair * width, width)].T
        for i in range(2):
            low = block[i * BLOCK : i * BLOCK + HALF]
            high = block[i * BLOCK + HALF : (i + 1) * BLOCK]
            mine[2 * pair + i] = jnp.where(core == 0, low, high)
            send[2 * pair + i] = jnp.where(core == 0, high, low)
    ids = rows[...]
    alive = lax.broadcasted_iota(jnp.int32, ids.shape, 1) < count[0]
    note[...] = jnp.zeros(note.shape, jnp.float32)
    note[0:1, : ids.shape[1]] = (ids >> 4).astype(jnp.float32)
    note[1:2, : ids.shape[1]] = jnp.where(alive, (ids & blocks_here - 1) + 1, 0).astype(jnp.float32)
    send[blocks_here] = note[...].astype(send.dtype)


def front(amplitudes, rows, count, here):
    lanes, columns = amplitudes.shape
    blocks_here = columns // BLOCK
    vmem = pl.BlockSpec(memory_space=pltpu.VMEM)
    smem = pl.BlockSpec(memory_space=pltpu.SMEM)
    return pl.pallas_call(
        front_kernel,
        out_shape=(
            jax.ShapeDtypeStruct((blocks_here, HALF, lanes), amplitudes.dtype),
            jax.ShapeDtypeStruct((blocks_here + 1, HALF, lanes), amplitudes.dtype),
        ),
        in_specs=[smem, smem, vmem, vmem],
        out_specs=(vmem, vmem),
        scratch_shapes=[pltpu.VMEM((HALF, lanes), jnp.float32)],
        compiler_params=LIMIT,
        cost_estimate=pl.CostEstimate(flops=0, bytes_accessed=4 * amplitudes.size, transcendentals=0),
    )(here, count, amplitudes, rows)


def requests_kernel(here, own, other, ask, place):
    core = here[0] & 1
    z = here[0] >> 1 & NZ - 1
    y = here[0] >> 4
    members, _, lanes = ask.shape
    per_member = NCORE * STEPS * NCORE * CAP
    square = (lanes, lanes)
    down = lax.broadcasted_iota(jnp.int32, square, 0)
    along = lax.broadcasted_iota(jnp.int32, square, 1)
    total = jnp.zeros((members, lanes), jnp.float32)
    for turn, note in enumerate((own[...], other[other.shape[0] - 1])):
        device = core if turn == 0 else 1 - core
        values = note.astype(jnp.float32)
        owner = values[0:1].astype(jnp.int32)
        index = values[1:2]
        wide = jnp.broadcast_to(values[0:1], square)
        live = jnp.broadcast_to(index, square)
        earlier = (wide.T == wide) & (down < along) & (live.T > 0.5)
        rank = jnp.sum(jnp.where(earlier, 1.0, 0.0), axis=0, keepdims=True).astype(jnp.int32)
        owner_z = owner >> 1 & NZ - 1
        owner_y = owner >> 4
        server = jnp.where(core == 0, owner_z, owner_y * 2 + (owner_z & 1))
        step = jnp.where(core == 0, owner_y - y, (owner_z >> 1) - (z >> 1)) & STEPS - 1
        within = ((device * STEPS + step) * NCORE + (owner & 1 ^ core)) * CAP + rank
        spot = server * per_member + within
        place[turn : turn + 1, :] = jnp.minimum(spot, members * per_member - 1)
        rows = lax.broadcasted_iota(jnp.int32, (members, lanes), 0)
        asked = jnp.where(rows == server, jnp.broadcast_to(index, (members, lanes)), 0.0)
        slot = jnp.where(down == within, 1.0, 0.0)
        total += lax.dot_general(
            asked.astype(jnp.bfloat16),
            slot.astype(jnp.bfloat16),
            (((1,), (1,)), ((), ())),
            preferred_element_type=jnp.float32,
        )
    found = total.astype(jnp.int32)
    for member in range(members):
        ask[member] = jnp.broadcast_to(found[member : member + 1], ask.shape[1:])


def requests(own, other, here):
    lanes = own.shape[-1]
    vmem = pl.BlockSpec(memory_space=pltpu.VMEM)
    return pl.pallas_call(
        requests_kernel,
        out_shape=(
            jax.ShapeDtypeStruct((MEMBERS, 1, lanes), jnp.int32),
            jax.ShapeDtypeStruct((8, lanes), jnp.int32),
        ),
        in_specs=[pl.BlockSpec(memory_space=pltpu.SMEM), vmem, vmem],
        out_specs=(vmem, vmem),
        compiler_params=LIMIT,
        cost_estimate=pl.CostEstimate(flops=0, bytes_accessed=65536, transcendentals=0),
    )(here, own, other)


def stack_kernel(mine, tiles, keep, out, buf, sem):
    slots, cols = keep.shape
    chunks, _, width = buf.shape
    each = slots // chunks

    def copy(i):
        return pltpu.make_async_copy(tiles.at[:, pl.ds(i * width, width)], buf.at[i], sem.at[i])

    for i in range(chunks):
        copy(i).start()
    for i in range(chunks):
        copy(i).wait()
        for part in range(2):
            half = mine[0] if part == 0 else 1 - mine[0]
            rows = pl.ds(pl.multiple_of(half * HALF, HALF), HALF)
            for j in range(each):
                s = i * each + j
                out[part, pl.ds(s * HALF, HALF), :] = (
                    buf[i, rows, pl.ds(j * cols, cols)] * keep[pl.ds(s, 1), :]
                )


def stack(mine, tiles, keep):
    slots, cols = keep.shape
    chunks = slots // GROUP
    return pl.pallas_call(
        stack_kernel,
        out_shape=jax.ShapeDtypeStruct((2, slots * HALF, cols), tiles.dtype),
        in_specs=[
            pl.BlockSpec(memory_space=pltpu.SMEM),
            pl.BlockSpec(memory_space=pl.ANY),
            pl.BlockSpec(memory_space=pltpu.VMEM),
        ],
        out_specs=pl.BlockSpec(memory_space=pltpu.VMEM),
        scratch_shapes=[
            pltpu.VMEM((chunks, BLOCK, GROUP * cols), tiles.dtype),
            pltpu.SemaphoreType.DMA((chunks,)),
        ],
        compiler_params=LIMIT,
        cost_estimate=pl.CostEstimate(
            flops=slots * BLOCK * cols, bytes_accessed=4 * slots * BLOCK * cols, transcendentals=0
        ),
    )(mine, tiles, keep)


def pick_kernel(asked, *refs):
    *sources, out = refs
    members = asked.shape[0]
    per_member = out.shape[0] // members
    blocks_here = sources[0].shape[0] // NCORE
    for member in range(members):
        for slot in range(per_member):
            step = slot % (STEPS * NCORE * CAP) // (NCORE * CAP)
            core = slot // CAP % NCORE
            block = jnp.maximum(asked[member, 0, slot] - 1, 0)
            out[member * per_member + slot] = sources[ORDER.index(step)][core * blocks_here + block]


def pick(asked, sources):
    members = asked.shape[0]
    slots = members * NCORE * STEPS * NCORE * CAP
    shape = (slots,) + sources[0].shape[1:]
    return pl.pallas_call(
        pick_kernel,
        out_shape=jax.ShapeDtypeStruct(shape, sources[0].dtype),
        in_specs=[pl.BlockSpec(memory_space=pltpu.SMEM)]
        + [pl.BlockSpec(memory_space=pltpu.VMEM)] * len(sources),
        out_specs=pl.BlockSpec(memory_space=pltpu.VMEM),
        compiler_params=LIMIT,
        cost_estimate=pl.CostEstimate(
            flops=0, bytes_accessed=4 * slots * HALF * shape[-1], transcendentals=0
        ),
    )(asked, *sources)


def select_kernel(place, blocks, out):
    for s in range(out.shape[0]):
        out[s] = blocks[place[1, s]]


def select(place, blocks, slots):
    shape = (slots,) + blocks.shape[1:]
    return pl.pallas_call(
        select_kernel,
        out_shape=jax.ShapeDtypeStruct(shape, blocks.dtype),
        in_specs=[
            pl.BlockSpec(memory_space=pltpu.SMEM),
            pl.BlockSpec(memory_space=pltpu.VMEM),
        ],
        out_specs=pl.BlockSpec(memory_space=pltpu.VMEM),
        compiler_params=LIMIT,
        cost_estimate=pl.CostEstimate(
            flops=0, bytes_accessed=2 * blocks.size, transcendentals=0
        ),
    )(place, blocks)


def contract_half(blocks, weights, half, total):
    each = 2 * GROUP
    depth = each * HALF
    for g in range(weights.shape[1] // depth):
        lhs = jnp.concatenate([blocks(g * each + s) for s in range(each)], axis=0)
        total += lax.dot_general(
            lhs,
            weights[half, pl.ds(g * depth, depth), :],
            (((0,), (0,)), ((), ())),
            preferred_element_type=jnp.float32,
        )
    return total


def first_kernel(place, blocks, weights, out):
    out[...] = contract_half(
        lambda s: blocks[place[0, s]], weights, 0, jnp.zeros(out.shape, jnp.float32)
    )


def second_kernel(blocks, weights, start, out):
    out[...] = contract_half(lambda s: blocks[s], weights, 1, start[...])


def first(place, blocks, weights):
    _, depth, cols = weights.shape
    rows = blocks.shape[-1]
    vmem = pl.BlockSpec(memory_space=pltpu.VMEM)
    return pl.pallas_call(
        first_kernel,
        out_shape=jax.ShapeDtypeStruct((rows, cols), jnp.float32),
        in_specs=[pl.BlockSpec(memory_space=pltpu.SMEM), vmem, vmem],
        out_specs=vmem,
        compiler_params=LIMIT,
        cost_estimate=pl.CostEstimate(
            flops=2 * depth * rows * cols, bytes_accessed=4 * 1024 * 1024, transcendentals=0
        ),
    )(place, blocks, weights)


def second(blocks, weights, start):
    _, depth, cols = weights.shape
    vmem = pl.BlockSpec(memory_space=pltpu.VMEM)
    return pl.pallas_call(
        second_kernel,
        out_shape=jax.ShapeDtypeStruct(start.shape, start.dtype),
        in_specs=[vmem, vmem, vmem],
        out_specs=vmem,
        compiler_params=LIMIT,
        cost_estimate=pl.CostEstimate(
            flops=2 * depth * start.size, bytes_accessed=2 * 1024 * 1024, transcendentals=0
        ),
    )(blocks, weights, start)


def body(amplitudes, block_tiles, block_rows, tile_mask, block_counts):
    slots = block_rows.shape[-1]
    cols_here = tile_mask.shape[-1] * BLOCK
    rows = amplitudes.shape[0]
    n_red = lax.axis_size("red")
    groups = server_groups()
    here = lax.axis_index("col").astype(jnp.int32)
    core = here & 1
    here = here.reshape(1)

    mine, send = front(amplitudes, block_rows[0], block_counts[0], here)
    given = lax.ppermute(send, "col", swap_pairs())
    alive = jnp.arange(slots) < block_counts[0, 0]
    keep = jnp.repeat(tile_mask[0, 0] * alive[:, None], BLOCK, axis=1).astype(jnp.bfloat16)
    given, keep = lax.optimization_barrier((given, keep))
    chip = jnp.concatenate([mine, given[:-1]])
    sources = [chip] + [lax.ppermute(chip, "col", step_pairs(s)) for s in ORDER[1:]]

    ask, place = requests(send[-1], given, here)
    asked = lax.all_to_all(
        ask, "col", split_axis=0, concat_axis=0, tiled=True, axis_index_groups=groups
    )

    weights = stack(core.reshape(1), block_tiles[0, 0], keep)
    asked, weights = lax.optimization_barrier((asked, weights))
    outgoing = pick(asked, sources)
    incoming = lax.all_to_all(
        outgoing.reshape(MEMBERS, -1, HALF, rows),
        "col",
        split_axis=0,
        concat_axis=0,
        tiled=True,
        axis_index_groups=groups,
    ).reshape(-1, HALF, rows)

    received = lax.ppermute(select(place, incoming, slots), "col", swap_pairs())
    partial_value = second(received, weights, first(place, incoming, weights))

    slices = partial_value.reshape(n_red, rows // n_red, cols_here)
    gathered = lax.all_to_all(slices, "red", split_axis=0, concat_axis=0, tiled=True)
    mine = jnp.sum(gathered, axis=0)
    copies = jnp.broadcast_to(mine[None], gathered.shape)
    whole = lax.all_to_all(copies, "red", split_axis=0, concat_axis=0, tiled=True)
    return whole.reshape(rows, cols_here)


def solution(mesh):
    placed = (
        P(None, ("red", "col")),
        P("red", "col", None, None),
        P("red", "col", None),
        P("red", "col", None, None),
        P("red", "col"),
    )
    return jax.shard_map(
        body, mesh=mesh, in_specs=placed, out_specs=P(None, "col"), check_vma=False
    )
```
